1024 devices in a mesh: blk: 64 (over x_lo, z, core), group: 16 (over y, x_hi).
Axes of the slice: x: 4 (x_hi: 2, x_lo: 2; x = x_hi * 2 + x_lo), y: 8, z: 16, core: 2. Of those that a mesh axis runs over, the one named last changes fastest.
Arguments:
- patches: bfloat16 [385024, 1152], P(('blk', 'group')), may hold values from -6 to 6
- patch_counts: int32 [1024, 16], P(('blk', 'group')), may hold values from 1 to 31, as said below
- dest_list: int32 [1024, 16], P(('blk', 'group')), may hold values from 0 to 15, as said below
- probe: bfloat16 [1152], replicated, may hold values from -900 to 900
- w_attn_out: bfloat16 [1152, 1152], replicated, may hold values from -0.1875 to 0.1875
- w_key: bfloat16 [1152, 1152], replicated, may hold values from -0.1875 to 0.1875
- w_value: bfloat16 [1152, 1152], replicated, may hold values from -0.1875 to 0.1875
- texts: bfloat16 [16384, 1152], P(('blk', 'group')), may hold values from -6 to 6
- image_labels: int32 [16384], P(('blk', 'group')), may hold values from 0 to 255
- text_labels: int32 [16384], P(('blk', 'group')), may hold values from 0 to 255
- log_temp: float32 [1], replicated, may hold values from 4 to 4.8
- bias: float32 [1], replicated, may hold values from -4 to -2
Outputs:
- image_grad: bfloat16 [16384, 1152], P(('blk', 'group'))
- text_grad: bfloat16 [16384, 1152], P(('blk', 'group'))
- row_loss: float32 [16384], P(('blk', 'group'))
The draws below stay inside these ranges and needn't reach their ends.
Inputs may be any that keep to these rules, and one draw needn't show every extreme that they name: `patch_counts`: one device's counts sum to at most 376, reached by a device of every block of 16 devices; the images that the devices of one such block send to one device (by dest_list) hold exactly 256 rows together. `dest_list`: each row names every device index of the group exactly once.
All inputs are finite; a program needn't handle non-finite values.
Results may differ from the reference program's by a relative error of at most 0.019.
Values may be sent and summed in bfloat16 or wider, within the bound.
A program may use at most 64 MiB of HBM per device.

```python
import jax
import jax.numpy as jnp
from jax import lax

D = 1152
HEADS = 16
ROW_UNIT = 1
HEAD = 72
IMG_DEV = 16
CAP_SRC = 376
TEXTS_COL = 1024
IMAGES = 16384
TOTAL_ROWS = 385024
LABELS = 256
N_BLK = 64
N_GROUP = 16


def layout_draw(key):
    first, second, third = jax.random.split(key, 3)
    iota = jnp.arange(N_GROUP, dtype=jnp.int32)

    def orders(stream_key, lead):
        ranks = jax.random.randint(stream_key, (lead, N_GROUP), 0, 1 << 20) * N_GROUP + iota[None, :]
        return jnp.argsort(ranks, axis=-1).astype(jnp.int32)
    dest = orders(first, N_BLK * N_GROUP).reshape(N_BLK, N_GROUP, N_GROUP)
    level_src = orders(second, N_BLK)
    level_dst = orders(third, N_BLK)
    where = (dest + iota[None, :, None]) % N_GROUP
    table = jnp.broadcast_to(level_dst[:, None, :], (N_BLK, N_GROUP, N_GROUP))
    extra = jnp.take_along_axis(table, where, axis=2)
    counts = ROW_UNIT * (level_src[:, :, None] + 1 + extra)
    return (dest.reshape(N_BLK * N_GROUP, N_GROUP).astype(jnp.int32), counts.reshape(N_BLK * N_GROUP, N_GROUP).astype(jnp.int32))


def draw_dest_list(key, part):
    return layout_draw(key)[0]


def draw_patch_counts(key, part):
    return layout_draw(key)[1]


def draw_probe(key, part):
    key = jax.random.fold_in(key, 5)
    first = jax.random.fold_in(key, 0)
    base = jnp.clip(jax.random.normal(first, (D,), jnp.float32), -6.0, 6.0)
    values = base
    return values.astype(jnp.bfloat16)


def with_ends(values, key, smallest, largest):
    place = [jax.random.randint(jax.random.fold_in(key, axis), (), 0, length) for axis, length in enumerate(values.shape)]
    longest = values.shape.index(max(values.shape))
    beside = place[:longest] + [(place[longest] + 1) % values.shape[longest]] + place[longest + 1:]
    return values.at[tuple(place)].set(smallest).at[tuple(beside)].set(largest)


def levels(key, extent, cuts, low, top_value):
    def one(axis_at, blocks):
        draws = jax.random.uniform(jax.random.fold_in(jax.random.fold_in(key, 6), axis_at), (blocks,), jnp.float32, low / len(cuts), top_value / len(cuts))
        return jnp.repeat(jnp.exp(draws), extent[axis_at] // blocks).reshape((-1,) + (1,) * (len(extent) - axis_at - 1))

    level = one(*cuts[0])
    for cut in cuts[1:]:
        level = level * one(*cut)
    return level


def bell_draw(rng, extent, scale, limit, cuts=(), held_as=jnp.bfloat16):
    loudness = levels(rng, extent, cuts, -0.22, 0.18) if cuts else 1.0
    entries = jax.random.normal(rng, extent, jnp.float32) * scale * loudness
    return jnp.minimum(jnp.maximum(entries, -limit), limit).astype(held_as)


def setup_inputs(seed: int = 0) -> dict:
    keys = jax.random.split(jax.random.key(seed), 13)
    return {
        "patches": bell_draw(keys[0], (TOTAL_ROWS, D), 1.0, 6.0, ((0, 1024),)),
        "patch_counts": draw_patch_counts(jax.random.fold_in(keys[12], 71), 0),
        "dest_list": draw_dest_list(jax.random.fold_in(keys[12], 71), 0),
        "probe": draw_probe(jax.random.fold_in(keys[12], 71), 0),
        "w_attn_out": bell_draw(keys[4], (D, D), D ** -0.5, 0.1875),
        "w_key": bell_draw(keys[5], (D, D), D ** -0.5, 0.1875),
        "w_value": bell_draw(keys[6], (D, D), D ** -0.5, 0.1875),
        "texts": bell_draw(keys[7], (IMAGES, D), 1.0, 6.0, ((0, 1024),)),
        "image_labels": with_ends(jax.random.randint(keys[8], (IMAGES,), 0, LABELS), jax.random.fold_in(keys[8], 1), 0, LABELS - 1).astype(jnp.int32),
        "text_labels": with_ends(jax.random.randint(keys[9], (IMAGES,), 0, LABELS), jax.random.fold_in(keys[9], 1), 0, LABELS - 1).astype(jnp.int32),
        "log_temp": jnp.clip(jax.random.uniform(keys[10], (1,), jnp.float32, 4.0, 4.8), 4.0, 4.8),
        "bias": jnp.clip(jax.random.uniform(keys[11], (1,), jnp.float32, -4.0, -2.0), -4.0, -2.0),
    }


def pool_rows(rows, segment, w_attn_out, key_probe, w_value, count):
    proj = jnp.dot(rows, w_attn_out, preferred_element_type=jnp.float32)
    centre = proj - lax.optimization_barrier(jnp.mean(proj, axis=-1, keepdims=True))
    normed = centre / jnp.sqrt(lax.optimization_barrier(jnp.mean(centre * centre, axis=-1, keepdims=True)) + 1e-06)
    scores = jnp.dot(normed, key_probe, precision=lax.Precision.HIGHEST) / jnp.sqrt(jnp.float32(HEAD))
    member = segment[None, :] == jnp.arange(count, dtype=jnp.int32)[:, None]
    masked = jnp.where(member[:, :, None], scores[None, :, :], -1e+30)
    top = lax.optimization_barrier(jnp.max(masked, axis=1, keepdims=True))
    expo = jnp.exp(masked - top) * member[:, :, None]
    weights = expo / lax.optimization_barrier(jnp.sum(expo, axis=1, keepdims=True))
    mixed = jnp.einsum('irh,rd->ihd', weights, normed, precision=lax.Precision.HIGHEST)
    pooled = jnp.einsum('ihd,dhe->ihe', mixed, w_value.astype(jnp.float32).reshape(D, HEADS, HEAD), precision=lax.Precision.HIGHEST)
    return pooled.reshape(count, D).astype(jnp.bfloat16)

def unit_rows(data):
    norm = jnp.sqrt(lax.optimization_barrier(jnp.sum(data * data, axis=-1, keepdims=True)) + 1e-06)
    return (data / norm, norm)

def reference(patches, patch_counts, dest_list, probe, w_attn_out, w_key, w_value, texts, image_labels, text_labels, log_temp, bias):
    devices = N_BLK * N_GROUP
    key_probe = lax.optimization_barrier(jnp.sum(w_key.astype(jnp.float32).reshape(D, HEADS, HEAD) * probe.astype(jnp.float32).reshape(HEADS, HEAD), axis=-1))
    slots = jnp.arange(CAP_SRC, dtype=jnp.int32)

    def one_device(item):
        rows, counts = item
        ends = jnp.cumsum(counts)
        segment = lax.optimization_barrier(jnp.sum((slots[:, None] >= ends[None, :]).astype(jnp.int32), axis=1)).astype(jnp.int32)
        return pool_rows(rows, segment, w_attn_out, key_probe, w_value, IMG_DEV)
    pooled = lax.map(one_device, (patches.reshape(devices, CAP_SRC, D), patch_counts))
    inverse = jnp.argsort(dest_list, axis=-1).astype(jnp.int32).reshape(N_BLK, N_GROUP, IMG_DEV)
    source = pooled.reshape(N_BLK, N_GROUP, IMG_DEV, D)
    chosen = jnp.take_along_axis(source, inverse[..., None], axis=2)
    placed = chosen.transpose(0, 2, 1, 3).reshape(IMAGES, D)
    image_unit, image_norm = unit_rows(placed.astype(jnp.float32))
    text_unit, text_norm = unit_rows(texts.astype(jnp.float32))
    image_keys = image_unit.astype(jnp.bfloat16)
    text_keys = text_unit.astype(jnp.bfloat16)

    def columns(data):
        return data.reshape(N_BLK, N_GROUP, IMG_DEV, *data.shape[1:]).swapaxes(0, 1).reshape(N_GROUP, TEXTS_COL, *data.shape[1:])

    def uncolumns(data):
        return data.reshape(N_GROUP, N_BLK, IMG_DEV, *data.shape[2:]).swapaxes(0, 1).reshape(IMAGES, *data.shape[2:])
    image_col = columns(image_keys).astype(jnp.float32)
    text_col = columns(text_keys).astype(jnp.float32)
    temp = jnp.exp(log_temp[0])
    logits = temp * jnp.einsum('gid,gjd->gij', image_col, text_col) + bias[0]
    signs = jnp.where(columns(image_labels)[:, :, None] == columns(text_labels)[:, None, :], 1.0, -1.0).astype(jnp.float32)
    row_loss = lax.optimization_barrier(jnp.sum(jax.nn.softplus(-signs * logits), axis=2)) / TEXTS_COL
    pair_weights = (temp * -signs * jax.nn.sigmoid(-signs * logits)).astype(jnp.bfloat16).astype(jnp.float32)
    grad_image_unit = uncolumns(jnp.einsum('gij,gjd->gid', pair_weights, text_col))
    grad_text_unit = uncolumns(jnp.einsum('gij,gid->gjd', pair_weights, image_col))
    image_grad = (grad_image_unit - image_unit * lax.optimization_barrier(jnp.sum(image_unit * grad_image_unit, axis=-1, keepdims=True))) / image_norm
    text_grad = (grad_text_unit - text_unit * lax.optimization_barrier(jnp.sum(text_unit * grad_text_unit, axis=-1, keepdims=True))) / text_norm
    return (image_grad.astype(jnp.bfloat16), text_grad.astype(jnp.bfloat16), uncolumns(row_loss))
```

```python
import functools

import jax
import jax.numpy as jnp
from jax import lax
from jax.experimental import pallas as pl
from jax.experimental.pallas import tpu as pltpu
from jax.sharding import PartitionSpec as P

HEADS = 16
LANES = 128
NEG = -1e30
F32 = jnp.float32
BF16 = jnp.bfloat16
NT = (((1,), (1,)), ((), ()))
TN = (((0,), (0,)), ((), ()))


def offsets(depth):
    if depth == 16:
        return ((0, 1, -1, 2), (0, 1, -1, -2), (0, 4, -4, 8))
    if depth == 4:
        return ((0, 1), (0, -1), (0, 2))
    raise ValueError("depth of z")


def dot(a, b, dims=(((1,), (0,)), ((), ()))):
    return lax.dot_general(a, b, dims, preferred_element_type=F32)


def split(data, pieces):
    out = []
    for _ in range(pieces - 1):
        piece = data.astype(BF16)
        out.append(piece)
        data = data - piece.astype(F32)
    return out + [data.astype(BF16)]


def iota(shape, axis):
    return lax.broadcasted_iota(jnp.int32, shape, axis)


def column(row):
    n = row.shape[1]
    same = iota((n, n), 0) == iota((n, n), 1)
    return jnp.sum(jnp.where(same, jnp.broadcast_to(row, (n, n)), 0.0), axis=1, keepdims=True)


def unit(data):
    norm = jnp.sqrt(jnp.sum(data * data, axis=-1, keepdims=True) + 1e-06)
    return (data / norm, norm)


def back(grad, row_unit, norm):
    return (grad - row_unit * jnp.sum(row_unit * grad, axis=-1, keepdims=True)) / norm


def pool(patch, counts, probe, key_w, proj_w, value_w, ready, normed):
    rows, width = patch.shape
    padded = normed.shape[0]
    head = width // HEADS
    images = counts.shape[1]
    ready("proj")
    proj = dot(patch[...], proj_w[...])
    centre = proj - jnp.mean(proj, axis=-1, keepdims=True)
    normed[0:rows, :] = centre / jnp.sqrt(jnp.mean(centre * centre, axis=-1, keepdims=True) + 1e-06)
    if padded > rows:
        normed[rows:padded, :] = jnp.zeros((padded - rows, width), F32)
    ready("key")
    low = iota((HEADS, width), 0) * head
    lane = iota((HEADS, width), 1)
    spread = jnp.where(
        (lane >= low) & (lane < low + head), jnp.broadcast_to(probe[...].astype(F32), (HEADS, width)), 0.0
    ).astype(BF16)
    key_probe = jnp.concatenate(split(dot(spread, key_w[...], NT), 3), axis=0)
    pieces = split(normed[...], 3)
    scores = jnp.zeros((HEADS, padded), F32)
    for at in (2, 1, 0):
        part = dot(key_probe[: HEADS * (3 - at)], pieces[at], NT)
        for piece in reversed(range(3 - at)):
            scores = scores + part[HEADS * piece : HEADS * (piece + 1)]
    scores = scores / jnp.sqrt(F32(head))
    both = images * HEADS
    image = iota((both, images), 0) // HEADS
    which = iota((both, images), 1)
    lengths = jnp.broadcast_to(counts[...].astype(F32), (both, images))
    first = jnp.sum(jnp.where(which < image, lengths, 0.0), axis=1, keepdims=True)
    last = jnp.sum(jnp.where(which <= image, lengths, 0.0), axis=1, keepdims=True)
    place = iota((both, padded), 1).astype(F32)
    member = (place >= first) & (place < last)
    masked = jnp.where(member, jnp.concatenate([scores] * images, axis=0), NEG)
    expo = jnp.where(member, jnp.exp(masked - jnp.max(masked, axis=1, keepdims=True)), 0.0)
    weights = split(expo / jnp.sum(expo, axis=1, keepdims=True), 2)
    mixed = dot(weights[0], pieces[0]) + (dot(weights[1], pieces[0]) + dot(weights[0], pieces[1]))
    ready("value")
    mixed = split(mixed, 2)
    full = dot(mixed[0], value_w[...]) + dot(mixed[1], value_w[...])
    low = (iota((both, width), 0) % HEADS) * head
    lane = iota((both, width), 1)
    kept = jnp.where((lane >= low) & (lane < low + head), full, 0.0)
    return jnp.sum(kept.reshape(images, HEADS, width), axis=1).astype(BF16)


def pairs(images, texts, width, temp, shift):
    logits = temp * dot(images[:, :width], texts[:, :width], NT) + shift
    apart = dot(images[:, width:], texts[:, width:], NT)
    signs = jnp.where(jnp.abs(apart) < 0.5, 1.0, -1.0).astype(F32)
    turned = -signs * logits
    small = jnp.exp(-jnp.abs(turned))
    loss = jnp.maximum(turned, 0.0) + jnp.log1p(small)
    sigmoid = jnp.where(turned >= 0, 1.0, small) / (1.0 + small)
    return (temp * -signs * sigmoid).astype(BF16), jnp.sum(loss, axis=1, keepdims=True)


def kernel(
    depth,
    peers,
    patches,
    counts,
    dest,
    probe,
    w_proj,
    w_key,
    w_value,
    texts,
    image_labels,
    text_labels,
    log_temp,
    bias,
    image_out,
    text_out,
    loss_out,
    patch_buf,
    proj_buf,
    key_buf,
    value_buf,
    text_buf,
    normed,
    row_out,
    row_in,
    text_set,
    image_set,
    image_back,
    image_got,
    core_back,
    core_got,
    text_back,
    text_got,
    load_sem,
    row_send,
    row_recv,
    text_send,
    text_recv,
    image_send,
    image_recv,
    iback_send,
    iback_recv,
    tback_send,
    tback_recv,
    core_send,
    core_recv,
):
    width = patches.shape[1]
    size = text_buf.shape[0]
    own_far, other_far, text_far = offsets(depth)
    reach = [(0, far) for far in own_far] + [(1, far) for far in other_far]
    half = len(text_far) * size

    here = lax.axis_index("blk")
    mine = lax.axis_index("group")
    at_x, at_z, at_core = here // (2 * depth), (here // 2) % depth, here % 2

    def blk(turn_x, far, turn_core):
        x = (at_x + turn_x) % 2
        z = (at_z + far + depth) % depth
        core = (at_core + turn_core) % 2
        return {"blk": (x * depth + z) * 2 + core}

    def remote(src, dst, send, recv, device):
        copy = pltpu.make_async_remote_copy(
            src_ref=src,
            dst_ref=dst,
            send_sem=send,
            recv_sem=recv,
            device_id=device,
            device_id_type=pl.DeviceIdType.MESH,
        )
        copy.start()
        return copy

    loads = {}
    for at, (name, src, dst) in enumerate(
        (
            ("text", texts, text_buf),
            ("patch", patches, patch_buf),
            ("proj", w_proj, proj_buf),
            ("key", w_key, key_buf),
            ("value", w_value, value_buf),
        )
    ):
        loads[name] = pltpu.make_async_copy(src, dst, load_sem.at[at])
        loads[name].start()

    known = {(turn, far % depth, 0) for turn, away in reach for far in (away, -away)}
    known |= {(0, far % depth, 0) for away in text_far for far in (away, -away)}
    known |= {(0, 0, 1)}
    known -= {(0, 0, 0)}
    barrier = pltpu.get_barrier_semaphore()
    for partner in sorted(known):
        pl.semaphore_signal(barrier, inc=1, device_id=blk(*partner), device_id_type=pl.DeviceIdType.MESH)
    for step in range(1, peers):
        pl.semaphore_signal(
            barrier, inc=1, device_id={"group": (mine + step) % peers}, device_id_type=pl.DeviceIdType.MESH
        )

    def block(ref, at, count=1):
        return ref.at[pl.ds(at * size, count * size), :]

    lane = iota((size, LANES), 1)
    loads["text"].wait()
    text_unit, text_norm = unit(text_buf[...].astype(F32))
    text_set[0:size, 0:width] = text_unit.astype(BF16)
    text_label = column(text_labels[...].astype(F32))
    text_set[0:size, width:] = jnp.where(lane == 0, 1.0, jnp.where(lane == 1, -text_label, 0.0)).astype(BF16)

    loads["patch"].wait()
    started = []
    text_copies = []

    def ready(name):
        loads[name].wait()
        if name == "key":
            pl.semaphore_wait(barrier, len(known) + peers - 1)
            for at in range(1, len(text_far)):
                text_copies.append(
                    remote(
                        block(text_set, 0),
                        block(text_set, at),
                        text_send.at[at],
                        text_recv.at[at],
                        blk(0, text_far[at], 0),
                    )
                )

    pooled = pool(patch_buf, counts, probe, key_buf, proj_buf, value_buf, ready, normed)
    chosen = jnp.broadcast_to(dest[...], (peers, peers)) == iota((peers, peers), 0)
    ordered = dot(jnp.where(chosen, 1.0, 0.0).astype(BF16), pooled)
    for at in range(peers):
        row_out[at] = ordered[at : at + 1, :]
    row_copies = []
    for step in range(1, peers):
        to = (mine + step) % peers
        row_copies.append(
            remote(
                row_out.at[to], row_in.at[mine], row_send.at[step], row_recv.at[step], {"group": to}
            )
        )
    row_in[mine] = row_out[mine]

    for copy in text_copies:
        copy.wait_recv()
    text_copies.append(
        remote(
            text_set.at[pl.ds(0, half), :],
            text_set.at[pl.ds(half, half), :],
            text_send.at[0],
            text_recv.at[0],
            blk(0, 0, 1),
        )
    )

    for copy in row_copies:
        copy.wait_recv()
    placed = jnp.concatenate([row_in[at] for at in range(peers)], axis=0)
    image_unit, image_norm = unit(placed)
    image_set[0:size, 0:width] = image_unit.astype(BF16)
    image_label = column(image_labels[...].astype(F32))
    image_set[0:size, width:] = jnp.where(lane == 0, image_label, jnp.where(lane == 1, 1.0, 0.0)).astype(BF16)
    image_copies = []
    for at in range(1, len(reach)):
        image_copies.append(
            remote(
                block(image_set, 0),
                block(image_set, at),
                image_send.at[at],
                image_recv.at[at],
                blk(reach[at][0], reach[at][1], 0),
            )
        )
    text_copies[-1].wait_recv()
    for copy in image_copies:
        copy.wait_recv()

    temp = jnp.exp(log_temp[...])
    weights, loss = pairs(image_set[...], text_set[...], width, temp, bias[...])
    text_part = dot(weights, image_set[:, :width], TN)
    core_back[...] = text_part[half:].astype(BF16)
    core_copy = remote(core_back, core_got, core_send.at[0], core_recv.at[0], blk(0, 0, 1))
    image_part = dot(weights, text_set[:, :width])
    image_back[:, 0:width] = image_part.astype(BF16)
    loss_high, loss_low = split(loss, 2)
    wide = iota((len(reach) * size, LANES), 1)
    image_back[:, width:] = jnp.where(
        wide == 0, loss_high.astype(F32), jnp.where(wide == 1, loss_low.astype(F32), 0.0)
    ).astype(BF16)
    core_copy.wait_recv()
    text_sum = text_part[:half] + core_got[...].astype(F32)
    text_back[...] = text_sum.astype(BF16)
    back_copies = []
    for at in range(1, len(text_far)):
        back_copies.append(
            remote(
                block(text_back, at),
                block(text_got, at),
                tback_send.at[at],
                tback_recv.at[at],
                blk(0, -text_far[at], 0),
            )
        )
    iback_copies = []
    for at in range(1, len(reach)):
        iback_copies.append(
            remote(
                block(image_back, at),
                block(image_got, at),
                iback_send.at[at],
                iback_recv.at[at],
                blk(reach[at][0], -reach[at][1], 0),
            )
        )
    image_sum = image_part[:size]
    loss_sum = loss[:size]
    for at, copy in enumerate(iback_copies, 1):
        copy.wait_recv()
        image_sum = image_sum + image_got[at * size : (at + 1) * size, :width].astype(F32)
        tail = image_got[at * size : (at + 1) * size, width:].astype(F32)
        loss_sum = loss_sum + jnp.sum(tail, axis=1, keepdims=True)
    image_out[...] = back(image_sum, image_unit, image_norm).astype(BF16)
    loss_sum = loss_sum / F32(len(reach) * len(text_far) * 2 * size)
    same = iota((size, size), 0) == iota((size, size), 1)
    loss_out[...] = jnp.sum(jnp.where(same, jnp.broadcast_to(loss_sum, (size, size)), 0.0), axis=0, keepdims=True)
    total = text_sum[:size]
    for at, copy in enumerate(back_copies, 1):
        copy.wait_recv()
        total = total + text_got[at * size : (at + 1) * size, :].astype(F32)
    text_out[...] = back(total, text_unit, text_norm).astype(BF16)

    for copy in row_copies + text_copies + image_copies + iback_copies + back_copies + [core_copy]:
        copy.wait_send()


def solution(mesh):
    depth = mesh.shape["blk"] // 4
    peers = mesh.shape["group"]
    own_far, other_far, text_far = offsets(depth)
    blocks = len(own_far) + len(other_far)
    lines = len(text_far)

    def body(
        patches,
        patch_counts,
        dest_list,
        probe,
        w_attn_out,
        w_key,
        w_value,
        texts,
        image_labels,
        text_labels,
        log_temp,
        bias,
    ):
        rows, width = patches.shape
        size = texts.shape[0]
        padded = -(-rows // LANES) * LANES
        far = pl.BlockSpec(memory_space=pl.ANY)
        near = pl.BlockSpec(memory_space=pltpu.VMEM)
        dma = lambda n: pltpu.SemaphoreType.DMA((n,))
        image_grad, text_grad, row_loss = pl.pallas_call(
            functools.partial(kernel, depth, peers),
            out_shape=(
                jax.ShapeDtypeStruct((size, width), BF16),
                jax.ShapeDtypeStruct((size, width), BF16),
                jax.ShapeDtypeStruct((1, size), F32),
            ),
            in_specs=[far, near, near, near, far, far, far, far, near, near, near, near],
            out_specs=(near, near, near),
            scratch_shapes=[
                pltpu.VMEM((rows, width), BF16),
                pltpu.VMEM((width, width), BF16),
                pltpu.VMEM((width, width), BF16),
                pltpu.VMEM((width, width), BF16),
                pltpu.VMEM((size, width), BF16),
                pltpu.VMEM((padded, width), F32),
                pltpu.VMEM((peers, 1, width), F32),
                pltpu.VMEM((peers, 1, width), F32),
                pltpu.VMEM((2 * lines * size, width + LANES), BF16),
                pltpu.VMEM((blocks * size, width + LANES), BF16),
                pltpu.VMEM((blocks * size, width + LANES), BF16),
                pltpu.VMEM((blocks * size, width + LANES), BF16),
                pltpu.VMEM((lines * size, width), BF16),
                pltpu.VMEM((lines * size, width), BF16),
                pltpu.VMEM((lines * size, width), BF16),
                pltpu.VMEM((lines * size, width), BF16),
                dma(5),
                dma(peers),
                dma(peers),
                dma(lines),
                dma(lines),
                dma(blocks),
                dma(blocks),
                dma(blocks),
                dma(blocks),
                dma(lines),
                dma(lines),
                dma(1),
                dma(1),
            ],
            compiler_params=pltpu.CompilerParams(
                collective_id=0, has_side_effects=True, vmem_limit_bytes=50 * 1024 * 1024
            ),
            cost_estimate=pl.CostEstimate(
                flops=8 * rows * width * width, bytes_accessed=8 * width * width, transcendentals=0
            ),
            name="pool_and_contrast",
        )(
            patches,
            patch_counts,
            dest_list,
            probe.reshape(1, width),
            w_attn_out,
            w_key,
            w_value,
            texts,
            image_labels.reshape(1, size),
            text_labels.reshape(1, size),
            log_temp.reshape(1, 1),
            bias.reshape(1, 1),
        )
        return (image_grad, text_grad, row_loss.reshape(size))

    whole = P(("blk", "group"), None)
    flat = P(("blk", "group"))
    return jax.shard_map(
        body,
        mesh=mesh,
        in_specs=(whole, whole, whole, P(), P(), P(), P(), whole, flat, flat, P(), P()),
        out_specs=(whole, whole, flat),
        check_vma=False,
    )
```

```python
import functools

import jax
import jax.numpy as jnp
from jax import lax
from jax.experimental import pallas as pl
from jax.experimental.pallas import tpu as pltpu
from jax.sharding import PartitionSpec as P

HEADS = 16
LANES = 128
NEG = -1e30
F32 = jnp.float32
BF16 = jnp.bfloat16
NT = (((1,), (1,)), ((), ()))
TN = (((0,), (0,)), ((), ()))


def offsets(depth):
    if depth == 16:
        return ((0, 1, -1, 2), (0, 4, -4, 8))
    if depth == 4:
        return ((0, 1), (0, 2))
    raise ValueError("depth of z")


def parts(width):
    return 3 if width % (3 * LANES) == 0 else 1


def dot(a, b, dims=(((1,), (0,)), ((), ()))):
    return lax.dot_general(a, b, dims, preferred_element_type=F32)


def split(data, pieces):
    out = []
    for _ in range(pieces - 1):
        piece = data.astype(BF16)
        out.append(piece)
        data = data - piece.astype(F32)
    return out + [data.astype(BF16)]


def iota(shape, axis):
    return lax.broadcasted_iota(jnp.int32, shape, axis)


def column(row):
    n = row.shape[1]
    same = iota((n, n), 0) == iota((n, n), 1)
    return jnp.sum(jnp.where(same, jnp.broadcast_to(row, (n, n)), 0.0), axis=1, keepdims=True)


def unit(data):
    norm = jnp.sqrt(jnp.sum(data * data, axis=-1, keepdims=True) + 1e-06)
    return (data / norm, norm)


def back(grad, row_unit, norm):
    return (grad - row_unit * jnp.sum(row_unit * grad, axis=-1, keepdims=True)) / norm


def pool(patch, counts, probe, key_w, proj_w, value_w, ready, normed):
    rows, width = patch.shape
    padded = normed.shape[0]
    head = width // HEADS
    images = counts.shape[1]
    cuts = parts(width)
    wide = width // cuts
    if padded > rows:
        normed[rows:padded, :] = jnp.zeros((padded - rows, width), F32)
    for cut in range(cuts):
        ready("proj", cut)
        normed[0:rows, cut * wide : (cut + 1) * wide] = dot(patch[...], proj_w[:, cut * wide : (cut + 1) * wide])
    proj = normed[0:rows, :]
    centre = proj - jnp.mean(proj, axis=-1, keepdims=True)
    normed[0:rows, :] = centre / jnp.sqrt(jnp.mean(centre * centre, axis=-1, keepdims=True) + 1e-06)
    low = iota((HEADS, width), 0) * head
    lane = iota((HEADS, width), 1)
    key_probe = []
    for cut in range(cuts):
        ready("key", cut)
        spread = jnp.where(
            (lane >= low) & (lane < low + head), jnp.broadcast_to(probe[...].astype(F32).reshape(1, width), (HEADS, width)), 0.0
        ).astype(BF16)
        key_probe.append(dot(spread, key_w[cut * wide : (cut + 1) * wide, :], NT))
    key_probe = jnp.concatenate(split(jnp.concatenate(key_probe, axis=1), 3), axis=0)
    pieces = split(normed[...], 2)
    scores = jnp.zeros((HEADS, padded), F32)
    for at in (1, 0):
        part = dot(key_probe[: HEADS * (3 - at)], pieces[at], NT)
        for piece in reversed(range(3 - at)):
            scores = scores + part[HEADS * piece : HEADS * (piece + 1)]
    scores = scores / jnp.sqrt(F32(head))
    image = iota((images, images), 0)
    which = iota((images, images), 1)
    lengths = jnp.broadcast_to(counts[...].astype(F32), (images, images))
    first = jnp.sum(jnp.where(which < image, lengths, 0.0), axis=1, keepdims=True)
    last = jnp.sum(jnp.where(which <= image, lengths, 0.0), axis=1, keepdims=True)
    place = iota((images, padded), 1).astype(F32)
    member = ((place >= first) & (place < last))[None]
    masked = jnp.where(member, scores[:, None, :], NEG)
    expo = jnp.where(member, jnp.exp(masked - jnp.max(masked, axis=2, keepdims=True)), 0.0)
    weights = expo / jnp.sum(expo, axis=2, keepdims=True)
    weights = weights.reshape(HEADS * images, padded).astype(BF16)
    mixed = split(dot(weights, pieces[0]), 2)
    out = []
    for cut in range(cuts):
        ready("value", cut)
        first_head, last_head = cut * wide // head, -(-(cut + 1) * wide // head)
        taken = slice(first_head * images, last_head * images)
        both = (last_head - first_head) * images
        full = dot(
            jnp.concatenate([piece[taken] for piece in mixed], axis=0), value_w[:, cut * wide : (cut + 1) * wide]
        )
        full = full[:both] + full[both:]
        lane = iota((images, wide), 1) + cut * wide
        kept = jnp.zeros((images, wide), F32)
        for at in range(first_head, last_head):
            inside = (lane >= at * head) & (lane < at * head + head)
            kept = jnp.where(inside, full[(at - first_head) * images : (at - first_head + 1) * images], kept)
        out.append(kept)
    return jnp.concatenate(out, axis=1).astype(BF16)


def pairs(images, texts, width, temp, shift):
    logits = temp * dot(images[:, :width], texts[:, :width], NT) + shift
    apart = dot(images[:, width:], texts[:, width:], NT)
    signs = jnp.where(jnp.abs(apart) < 0.5, 1.0, -1.0).astype(F32)
    turned = -signs * logits
    small = jnp.exp(-jnp.abs(turned))
    loss = jnp.maximum(turned, 0.0) + jnp.log1p(small)
    sigmoid = jnp.where(turned >= 0, 1.0, small) / (1.0 + small)
    return (temp * -signs * sigmoid).astype(BF16), jnp.sum(loss, axis=1, keepdims=True)


def kernel(
    depth,
    peers,
    patches,
    counts_hbm,
    dest_hbm,
    probe_hbm,
    w_proj,
    w_key,
    w_value,
    texts,
    image_labels_hbm,
    text_labels_hbm,
    log_temp_hbm,
    bias_hbm,
    image_out,
    text_out,
    loss_out,
    counts,
    dest,
    probe,
    image_labels,
    text_labels,
    log_temp,
    bias,
    patch_buf,
    proj_buf,
    key_buf,
    value_buf,
    text_buf,
    normed,
    row_out,
    row_in,
    text_set,
    image_set,
    side_back,
    side_got,
    image_back,
    image_got,
    core_back,
    core_got,
    text_back,
    text_got,
    load_sem,
    row_send,
    row_recv,
    text_send,
    text_recv,
    image_send,
    image_recv,
    iback_send,
    iback_recv,
    tback_send,
    tback_recv,
    core_send,
    core_recv,
):
    width = patches.shape[1]
    size = text_buf.shape[0]
    image_far, text_far = offsets(depth)
    reach = [(turn, far) for turn in (0, 1) for far in image_far]
    half = len(text_far) * size
    near = len(image_far) * size

    here = lax.axis_index("blk")
    mine = lax.axis_index("group")
    at_x, at_z, at_core = here // (2 * depth), (here // 2) % depth, here % 2
    way = 1 - 2 * at_core

    def blk(turn_x, far, turn_core):
        x = (at_x + turn_x) % 2
        z = (at_z + far + depth) % depth
        core = (at_core + turn_core) % 2
        return {"blk": (x * depth + z) * 2 + core}

    def remote(src, dst, send, recv, device):
        copy = pltpu.make_async_remote_copy(
            src_ref=src,
            dst_ref=dst,
            send_sem=send,
            recv_sem=recv,
            device_id=device,
            device_id_type=pl.DeviceIdType.MESH,
        )
        copy.start()
        return copy

    loads = {}

    def load(name, src, dst):
        loads[name] = pltpu.make_async_copy(src, dst, load_sem.at[len(loads)])
        loads[name].start()

    cuts = parts(width)
    wide = width // cuts
    load("patch", patches, patch_buf)
    for cut in range(cuts):
        some = pl.ds(cut * wide, wide)
        load(("proj", cut), w_proj.at[:, some], proj_buf.at[:, some])
    load("text", texts, text_buf)
    for name, src, dst in (
        ("counts", counts_hbm, counts),
        ("dest", dest_hbm, dest),
        ("probe", probe_hbm, probe),
        ("image_labels", image_labels_hbm, image_labels),
        ("text_labels", text_labels_hbm, text_labels),
        ("log_temp", log_temp_hbm, log_temp),
        ("bias", bias_hbm, bias),
    ):
        load(name, src, dst)
    for cut in range(cuts):
        some = pl.ds(cut * wide, wide)
        load(("key", cut), w_key.at[some, :], key_buf.at[some, :])
    for cut in range(cuts):
        some = pl.ds(cut * wide, wide)
        load(("value", cut), w_value.at[:, some], value_buf.at[:, some])

    known = {(turn, far % depth, 0) for turn, away in reach for far in (away, -away)}
    known |= {(0, far % depth, 0) for away in text_far for far in (away, -away)}
    known |= {(0, 0, 1)}
    known -= {(0, 0, 0)}
    barrier = pltpu.get_barrier_semaphore()
    for partner in sorted(known):
        pl.semaphore_signal(barrier, inc=1, device_id=blk(*partner), device_id_type=pl.DeviceIdType.MESH)
    for step in range(1, peers):
        pl.semaphore_signal(
            barrier, inc=1, device_id={"group": (mine + step) % peers}, device_id_type=pl.DeviceIdType.MESH
        )

    def block(ref, at, count=1):
        return ref.at[pl.ds(at * size, count * size), :]

    lane = iota((size, LANES), 1)
    loads["patch"].wait()
    text_copies = []
    kept = {}

    def ready(name, cut):
        loads[(name, cut)].wait()
        if name == "key" and cut == 0:
            for other in ("text", "counts", "dest", "probe", "image_labels", "text_labels", "log_temp", "bias"):
                loads[other].wait()
            text_unit, text_norm = unit(text_buf[...].astype(F32))
            kept["text"] = (text_unit, text_norm)
            text_set[0:size, 0:width] = text_unit.astype(BF16)
            text_label = column(text_labels[...].astype(F32))
            text_set[0:size, width:] = jnp.where(lane == 0, 1.0, jnp.where(lane == 1, -text_label, 0.0)).astype(BF16)

    pooled = pool(patch_buf, counts, probe, key_buf, proj_buf, value_buf, ready, normed)
    chosen = jnp.broadcast_to(dest[...], (peers, peers)) == iota((peers, peers), 0)
    ordered = dot(jnp.where(chosen, 1.0, 0.0).astype(BF16), pooled)
    for at in range(peers):
        row_out[at] = ordered[at : at + 1, :]
    pl.semaphore_wait(barrier, len(known) + peers - 1)
    row_copies = []
    for step in sorted(range(1, peers), key=lambda step: abs(step - peers // 2)):
        to = (mine + step) % peers
        row_copies.append(
            remote(
                row_out.at[to], row_in.at[mine], row_send.at[step], row_recv.at[step], {"group": to}
            )
        )
    row_in[mine] = row_out[mine]
    for at in reversed(range(1, len(text_far))):
        text_copies.append(
            remote(
                block(text_set, 0),
                block(text_set, at),
                text_send.at[at],
                text_recv.at[at],
                blk(0, text_far[at], 0),
            )
        )

    for copy in row_copies:
        copy.wait_recv()
    placed = jnp.concatenate([row_in[at] for at in range(peers)], axis=0)
    image_unit, image_norm = unit(placed)
    image_set[0:size, 0:width] = image_unit.astype(BF16)
    image_label = column(image_labels[...].astype(F32))
    image_set[0:size, width:] = jnp.where(lane == 0, image_label, jnp.where(lane == 1, 1.0, 0.0)).astype(BF16)
    image_copies = []
    for at in sorted(range(1, len(reach)), key=lambda at: -abs(reach[at][1])):
        image_copies.append(
            remote(
                block(image_set, 0),
                block(image_set, at),
                image_send.at[at],
                image_recv.at[at],
                blk(reach[at][0], way * reach[at][1], 0),
            )
        )
    for copy in text_copies:
        copy.wait_recv()
    text_copies.append(
        remote(
            text_set.at[pl.ds(0, half), :],
            text_set.at[pl.ds(half, half), :],
            text_send.at[0],
            text_recv.at[0],
            blk(0, 0, 1),
        )
    )
    text_copies[-1].wait_recv()
    for copy in image_copies:
        copy.wait_recv()

    temp = jnp.exp(log_temp[...])
    weights, loss = pairs(image_set[...], text_set[...], width, temp, bias[...])
    text_part = dot(weights, image_set[:, :width], TN)
    core_back[...] = text_part[half:].astype(BF16)
    core_copy = remote(core_back, core_got, core_send.at[0], core_recv.at[0], blk(0, 0, 1))
    image_part = dot(weights, text_set[:, :width])
    wide_lane = iota((near, LANES), 1)

    def tails(data):
        high, low = split(data, 2)
        return jnp.where(
            wide_lane == 0, high.astype(F32), jnp.where(wide_lane == 1, low.astype(F32), 0.0)
        ).astype(BF16)

    def tail(data):
        return jnp.sum(data.astype(F32), axis=1, keepdims=True)

    side_back[:, 0:width] = image_part[near:].astype(BF16)
    side_back[:, width:] = tails(loss[near:])
    side_copy = remote(side_back, side_got, core_send.at[1], core_recv.at[1], blk(1, 0, 0))
    core_copy.wait_recv()
    text_sum = text_part[:half] + core_got[...].astype(F32)
    text_back[...] = text_sum.astype(BF16)
    back_copies = {}
    for at in reversed(range(1, len(text_far))):
        back_copies[at] = remote(
            block(text_back, at),
            block(text_got, at),
            tback_send.at[at],
            tback_recv.at[at],
            blk(0, -text_far[at], 0),
        )
    side_copy.wait_recv()
    image_sum = image_part[:near] + side_got[:, 0:width].astype(F32)
    loss_sum = loss[:near] + tail(side_got[:, width:])
    image_back[:, 0:width] = image_sum.astype(BF16)
    image_back[:, width:] = tails(loss_sum)
    iback_copies = {}
    for at in reversed(range(1, len(image_far))):
        iback_copies[at] = remote(
            block(image_back, at),
            block(image_got, at),
            iback_send.at[at],
            iback_recv.at[at],
            blk(0, -way * image_far[at], 0),
        )
    image_sum = image_sum[:size]
    loss_sum = loss_sum[:size]
    for at, copy in iback_copies.items():
        copy.wait_recv()
        image_sum = image_sum + image_got[at * size : (at + 1) * size, :width].astype(F32)
        loss_sum = loss_sum + tail(image_got[at * size : (at + 1) * size, width:])
    image_out[...] = back(image_sum, image_unit, image_norm).astype(BF16)
    loss_sum = loss_sum / F32(len(reach) * len(text_far) * 2 * size)
    same = iota((size, size), 0) == iota((size, size), 1)
    loss_out[...] = jnp.sum(jnp.where(same, jnp.broadcast_to(loss_sum, (size, size)), 0.0), axis=0, keepdims=True)
    text_unit, text_norm = kept["text"]
    total = text_sum[:size]
    for at, copy in back_copies.items():
        copy.wait_recv()
        total = total + text_got[at * size : (at + 1) * size, :].astype(F32)
    text_out[...] = back(total, text_unit, text_norm).astype(BF16)

    last = [core_copy, side_copy] + list(iback_copies.values()) + list(back_copies.values())
    for copy in row_copies + text_copies + image_copies + last:
        copy.wait_send()


def solution(mesh):
    depth = mesh.shape["blk"] // 4
    peers = mesh.shape["group"]
    image_far, text_far = offsets(depth)
    near = len(image_far)
    lines = len(text_far)

    def body(
        patches,
        patch_counts,
        dest_list,
        probe,
        w_attn_out,
        w_key,
        w_value,
        texts,
        image_labels,
        text_labels,
        log_temp,
        bias,
    ):
        rows, width = patches.shape
        size = texts.shape[0]
        padded = -(-rows // LANES) * LANES
        far = pl.BlockSpec(memory_space=pl.ANY)
        local = pl.BlockSpec(memory_space=pltpu.VMEM)
        dma = lambda n: pltpu.SemaphoreType.DMA((n,))
        image_grad, text_grad, row_loss = pl.pallas_call(
            functools.partial(kernel, depth, peers),
            out_shape=(
                pltpu.VMEM((size, width), BF16),
                pltpu.VMEM((size, width), BF16),
                pltpu.VMEM((1, size), F32),
            ),
            in_specs=[far] * 12,
            out_specs=(local, local, local),
            scratch_shapes=[
                pltpu.VMEM((1, peers), jnp.int32),
                pltpu.VMEM((1, peers), jnp.int32),
                pltpu.VMEM((width,), BF16),
                pltpu.VMEM((1, size), jnp.int32),
                pltpu.VMEM((1, size), jnp.int32),
                pltpu.VMEM((1, 1), F32),
                pltpu.VMEM((1, 1), F32),
                pltpu.VMEM((rows, width), BF16),
                pltpu.VMEM((width, width), BF16),
                pltpu.VMEM((width, width), BF16),
                pltpu.VMEM((width, width), BF16),
                pltpu.VMEM((size, width), BF16),
                pltpu.VMEM((padded, width), F32),
                pltpu.VMEM((peers, 1, width), F32),
                pltpu.VMEM((peers, 1, width), F32),
                pltpu.VMEM((2 * lines * size, width + LANES), BF16),
                pltpu.VMEM((2 * near * size, width + LANES), BF16),
                pltpu.VMEM((near * size, width + LANES), BF16),
                pltpu.VMEM((near * size, width + LANES), BF16),
                pltpu.VMEM((near * size, width + LANES), BF16),
                pltpu.VMEM((near * size, width + LANES), BF16),
                pltpu.VMEM((lines * size, width), BF16),
                pltpu.VMEM((lines * size, width), BF16),
                pltpu.VMEM((lines * size, width), BF16),
                pltpu.VMEM((lines * size, width), BF16),
                dma(9 + 3 * parts(width)),
                dma(peers),
                dma(peers),
                dma(lines),
                dma(lines),
                dma(2 * near),
                dma(2 * near),
                dma(near),
                dma(near),
                dma(lines),
                dma(lines),
                dma(2),
                dma(2),
            ],
            compiler_params=pltpu.CompilerParams(
                collective_id=0, has_side_effects=True, vmem_limit_bytes=62 * 1024 * 1024
            ),
            cost_estimate=pl.CostEstimate(
                flops=8 * rows * width * width, bytes_accessed=8 * width * width, transcendentals=0
            ),
            name="pool_and_contrast",
        )(
            patches,
            patch_counts,
            dest_list,
            probe,
            w_attn_out,
            w_key,
            w_value,
            texts,
            image_labels.reshape(1, size),
            text_labels.reshape(1, size),
            log_temp.reshape(1, 1),
            bias.reshape(1, 1),
        )
        return (image_grad, text_grad, row_loss.reshape(size))

    whole = P(("blk", "group"), None)
    flat = P(("blk", "group"))
    return jax.shard_map(
        body,
        mesh=mesh,
        in_specs=(whole, whole, whole, P(), P(), P(), P(), whole, flat, flat, P(), P()),
        out_specs=(whole, whole, flat),
        check_vma=False,
    )
```

```python
import functools

import jax
import jax.numpy as jnp
from jax import lax
from jax.experimental import pallas as pl
from jax.experimental.pallas import tpu as pltpu
from jax.sharding import PartitionSpec as P

HEADS = 16
LANES = 128
NEG = -1e30
F32 = jnp.float32
BF16 = jnp.bfloat16
NT = (((1,), (1,)), ((), ()))
TN = (((0,), (0,)), ((), ()))


def offsets(depth):
    if depth == 16:
        return ((0, 1, -1, 2), (-6, 6, -2, 2))
    if depth == 4:
        return ((0, 1), (-1, 1))
    raise ValueError("depth of z")


def parts(width):
    return 3 if width % (3 * LANES) == 0 else 1


def dot(a, b, dims=(((1,), (0,)), ((), ()))):
    return lax.dot_general(a, b, dims, preferred_element_type=F32)


def split(data, pieces):
    out = []
    for _ in range(pieces - 1):
        piece = data.astype(BF16)
        out.append(piece)
        data = data - piece.astype(F32)
    return out + [data.astype(BF16)]


def iota(shape, axis):
    return lax.broadcasted_iota(jnp.int32, shape, axis)


def column(row):
    n = row.shape[1]
    same = iota((n, n), 0) == iota((n, n), 1)
    return jnp.sum(jnp.where(same, jnp.broadcast_to(row, (n, n)), 0.0), axis=1, keepdims=True)


def unit(data):
    norm = jnp.sqrt(jnp.sum(data * data, axis=-1, keepdims=True) + 1e-06)
    return (data / norm, norm)


def back(grad, row_unit, norm):
    return (grad - row_unit * jnp.sum(row_unit * grad, axis=-1, keepdims=True)) / norm


def pool(patch, counts, dest, probe, key_w, proj_w, value_w, ready, normed):
    rows, width = patch.shape
    padded = normed.shape[0]
    head = width // HEADS
    images = counts.shape[1]
    cuts = parts(width)
    wide = width // cuts
    if padded > rows:
        normed[rows:padded, :] = jnp.zeros((padded - rows, width), F32)
    for cut in range(cuts):
        ready("proj", cut)
        normed[0:rows, cut * wide : (cut + 1) * wide] = dot(patch[...], proj_w[:, cut * wide : (cut + 1) * wide])
    proj = normed[0:rows, :]
    centre = proj - jnp.mean(proj, axis=-1, keepdims=True)
    normed[0:rows, :] = centre / jnp.sqrt(jnp.mean(centre * centre, axis=-1, keepdims=True) + 1e-06)
    low = iota((HEADS, width), 0) * head
    lane = iota((HEADS, width), 1)
    key_probe = []
    for cut in range(cuts):
        ready("key", cut)
        spread = jnp.where(
            (lane >= low) & (lane < low + head), jnp.broadcast_to(probe[...].astype(F32).reshape(1, width), (HEADS, width)), 0.0
        ).astype(BF16)
        key_probe.append(dot(spread, key_w[cut * wide : (cut + 1) * wide, :], NT))
    key_probe = jnp.concatenate(split(jnp.concatenate(key_probe, axis=1), 3), axis=0)
    pieces = split(normed[...], 2)
    scores = jnp.zeros((HEADS, padded), F32)
    for at in (1, 0):
        part = dot(key_probe[: HEADS * (3 - at)], pieces[at], NT)
        for piece in reversed(range(3 - at)):
            scores = scores + part[HEADS * piece : HEADS * (piece + 1)]
    scores = scores / jnp.sqrt(F32(head))
    image = iota((images, images), 0)
    which = iota((images, images), 1)
    lengths = jnp.broadcast_to(column(counts[...].astype(F32)), (images, images))
    first = jnp.sum(jnp.where(image < which, lengths, 0.0), axis=0, keepdims=True)
    last = jnp.sum(jnp.where(image <= which, lengths, 0.0), axis=0, keepdims=True)
    chosen = jnp.broadcast_to(dest[...], (images, images)) == image
    first = jnp.sum(jnp.where(chosen, jnp.broadcast_to(first, (images, images)), 0.0), axis=1, keepdims=True)
    last = jnp.sum(jnp.where(chosen, jnp.broadcast_to(last, (images, images)), 0.0), axis=1, keepdims=True)
    place = iota((images, padded), 1).astype(F32)
    member = ((place >= first) & (place < last))[None]
    masked = jnp.where(member, scores[:, None, :], NEG)
    expo = jnp.where(member, jnp.exp(masked - jnp.max(masked, axis=2, keepdims=True)), 0.0)
    weights = expo / jnp.sum(expo, axis=2, keepdims=True)
    weights = weights.reshape(HEADS * images, padded).astype(BF16)
    mixed = split(dot(weights, pieces[0]), 2)
    out = []
    for cut in range(cuts):
        ready("value", cut)
        first_head, last_head = cut * wide // head, -(-(cut + 1) * wide // head)
        taken = slice(first_head * images, last_head * images)
        both = (last_head - first_head) * images
        full = dot(
            jnp.concatenate([piece[taken] for piece in mixed], axis=0), value_w[:, cut * wide : (cut + 1) * wide]
        )
        full = full[:both] + full[both:]
        lane = iota((images, wide), 1) + cut * wide
        kept = jnp.zeros((images, wide), F32)
        for at in range(first_head, last_head):
            inside = (lane >= at * head) & (lane < at * head + head)
            kept = jnp.where(inside, full[(at - first_head) * images : (at - first_head + 1) * images], kept)
        out.append(kept)
    return jnp.concatenate(out, axis=1).astype(BF16).astype(F32)


def pairs(images, texts, width, temp, shift):
    logits = temp * dot(images[:, :width], texts[:, :width], NT) + shift
    apart = dot(images[:, width:], texts[:, width:], NT)
    signs = jnp.where(jnp.abs(apart) < 0.5, 1.0, -1.0).astype(F32)
    turned = -signs * logits
    small = jnp.exp(-jnp.abs(turned))
    loss = jnp.maximum(turned, 0.0) + jnp.log1p(small)
    sigmoid = jnp.where(turned >= 0, 1.0, small) / (1.0 + small)
    return (temp * -signs * sigmoid).astype(BF16), jnp.sum(loss, axis=1, keepdims=True)


def kernel(
    depth,
    peers,
    patches,
    counts_hbm,
    dest_hbm,
    probe_hbm,
    w_proj,
    w_key,
    w_value,
    texts,
    image_labels_hbm,
    text_labels_hbm,
    log_temp,
    bias,
    image_out,
    text_out,
    loss_out,
    counts,
    dest,
    probe,
    image_labels,
    text_labels,
    patch_buf,
    proj_buf,
    key_buf,
    value_buf,
    text_buf,
    normed,
    row_out,
    row_in,
    text_own,
    text_set,
    image_set,
    side_back,
    side_got,
    image_back,
    image_got,
    core_back,
    core_got,
    text_back,
    text_got,
    load_sem,
    row_send,
    row_recv,
    text_send,
    text_recv,
    image_send,
    image_recv,
    iback_send,
    iback_recv,
    tback_send,
    tback_recv,
    core_send,
    core_recv,
    side_send,
    side_recv,
):
    width = patches.shape[1]
    size = text_buf.shape[0]
    image_far, text_far = offsets(depth)
    reach = [(turn, far) for turn in (0, 1) for far in image_far]
    half = len(text_far) * size
    near = len(image_far)

    here = lax.axis_index("blk")
    mine = lax.axis_index("group")
    at_x, at_z, at_core = here // (2 * depth), (here // 2) % depth, here % 2
    way = 1 - 2 * at_core

    def blk(turn_x, far, turn_core):
        x = (at_x + turn_x) % 2
        z = (at_z + far + depth) % depth
        core = (at_core + turn_core) % 2
        return {"blk": (x * depth + z) * 2 + core}

    def remote(src, dst, send, recv, device):
        copy = pltpu.make_async_remote_copy(
            src_ref=src,
            dst_ref=dst,
            send_sem=send,
            recv_sem=recv,
            device_id=device,
            device_id_type=pl.DeviceIdType.MESH,
        )
        copy.start()
        return copy

    loads = {}

    def load(name, src, dst):
        loads[name] = pltpu.make_async_copy(src, dst, load_sem.at[len(loads)])
        loads[name].start()

    cuts = parts(width)
    wide = width // cuts
    load("patch", patches, patch_buf)
    for cut in range(cuts):
        some = pl.ds(cut * wide, wide)
        load(("proj", cut), w_proj.at[:, some], proj_buf.at[:, some])
    load("text", texts, text_buf)
    for name, src, dst in (
        ("counts", counts_hbm, counts),
        ("dest", dest_hbm, dest),
        ("probe", probe_hbm, probe),
        ("image_labels", image_labels_hbm, image_labels),
        ("text_labels", text_labels_hbm, text_labels),
    ):
        load(name, src, dst)
    for cut in range(cuts):
        some = pl.ds(cut * wide, wide)
        load(("key", cut), w_key.at[some, :], key_buf.at[some, :])
    for cut in range(cuts):
        some = pl.ds(cut * wide, wide)
        load(("value", cut), w_value.at[:, some], value_buf.at[:, some])

    known = {(turn, far % depth, 0) for turn, away in reach for far in (away, -away)}
    known |= {(0, far % depth, 0) for away in text_far for far in (away, -away)}
    known |= {(0, 0, 1)}
    known -= {(0, 0, 0)}
    barrier = pltpu.get_barrier_semaphore()
    for partner in sorted(known):
        pl.semaphore_signal(barrier, inc=1, device_id=blk(*partner), device_id_type=pl.DeviceIdType.MESH)
    for step in range(1, peers):
        pl.semaphore_signal(
            barrier, inc=1, device_id={"group": (mine + step) % peers}, device_id_type=pl.DeviceIdType.MESH
        )

    def block(ref, at, count=1):
        return ref.at[pl.ds(at * size, count * size), :]

    lane = iota((size, LANES), 1)
    loads["patch"].wait()
    text_copies = []
    kept = {}

    def ready(name, cut):
        loads[(name, cut)].wait()
        if name == "key" and cut == 0:
            for other in ("text", "counts", "dest", "probe", "image_labels", "text_labels"):
                loads[other].wait()
            text_unit, text_norm = unit(text_buf[...].astype(F32))
            kept["text"] = (text_unit, text_norm)
            text_own[:, 0:width] = text_unit.astype(BF16)
            text_label = column(text_labels[...].astype(F32))
            text_own[:, width:] = jnp.where(lane == 0, 1.0, jnp.where(lane == 1, -text_label, 0.0)).astype(BF16)

    ordered = pool(patch_buf, counts, dest, probe, key_buf, proj_buf, value_buf, ready, normed)
    for at in range(peers):
        row_out[at] = ordered[at : at + 1, :]
    pl.semaphore_wait(barrier, len(known) + peers - 1)
    row_copies = []
    for step in sorted(range(1, peers), key=lambda step: abs(step - peers // 2)):
        to = (mine + step) % peers
        row_copies.append(
            remote(
                row_out.at[to], row_in.at[mine], row_send.at[step], row_recv.at[step], {"group": to}
            )
        )
    row_in[mine] = row_out[mine]
    for at in range(len(text_far)):
        text_copies.append(
            remote(
                text_own,
                block(text_set, at),
                text_send.at[at],
                text_recv.at[at],
                blk(0, text_far[at], 0),
            )
        )

    for copy in row_copies:
        copy.wait_recv()
    placed = jnp.concatenate([row_in[at] for at in range(peers)], axis=0)
    image_unit, image_norm = unit(placed)
    image_set[0:size, 0:width] = image_unit.astype(BF16)
    image_label = column(image_labels[...].astype(F32))
    image_set[0:size, width:] = jnp.where(lane == 0, image_label, jnp.where(lane == 1, 1.0, 0.0)).astype(BF16)
    image_copies = []
    for at in sorted(range(1, len(reach)), key=lambda at: -abs(reach[at][1])):
        image_copies.append(
            remote(
                block(image_set, 0),
                block(image_set, at),
                image_send.at[at],
                image_recv.at[at],
                blk(reach[at][0], way * reach[at][1], 0),
            )
        )
    for copy in text_copies:
        copy.wait_recv()
    text_copies.append(
        remote(
            text_set.at[pl.ds(0, half), :],
            text_set.at[pl.ds(half, half), :],
            text_send.at[len(text_far)],
            text_recv.at[len(text_far)],
            blk(0, 0, 1),
        )
    )
    text_copies[-1].wait_recv()
    for copy in image_copies:
        copy.wait_recv()

    temp = jnp.exp(jnp.full((1, 1), log_temp[0], F32))
    weights, loss = pairs(image_set[...], text_set[...], width, temp, jnp.full((1, 1), bias[0], F32))
    text_part = dot(weights, image_set[:, :width], TN)
    core_back[...] = text_part[half:].astype(BF16)
    core_copy = remote(core_back, core_got, core_send.at[0], core_recv.at[0], blk(0, 0, 1))
    image_part = dot(weights, text_set[:, :width])

    def tails(data):
        wide_lane = iota((data.shape[0], LANES), 1)
        high, low = split(data, 2)
        return jnp.where(
            wide_lane == 0, high.astype(F32), jnp.where(wide_lane == 1, low.astype(F32), 0.0)
        ).astype(BF16)

    def tail(data):
        return jnp.sum(data.astype(F32), axis=1, keepdims=True)

    side_back[:, 0:width] = image_part[near * size :].astype(BF16)
    side_back[:, width:] = tails(loss[near * size :])
    order = sorted(range(near), key=lambda at: -abs(image_far[at]))
    side_copies = {}
    for at in order:
        side_copies[at] = remote(
            block(side_back, at), block(side_got, at), side_send.at[at], side_recv.at[at], blk(1, 0, 0)
        )
    core_copy.wait_recv()
    text_sum = text_part[:half] + core_got[...].astype(F32)
    text_back[...] = text_sum.astype(BF16)
    back_copies = {}
    for at in range(len(text_far)):
        back_copies[at] = remote(
            block(text_back, at),
            block(text_got, at),
            tback_send.at[at],
            tback_recv.at[at],
            blk(0, -text_far[at], 0),
        )
    iback_copies = {}
    for at in order:
        side_copies[at].wait_recv()
        rows = slice(at * size, (at + 1) * size)
        image_sum = image_part[rows] + side_got[rows, 0:width].astype(F32)
        loss_sum = loss[rows] + tail(side_got[rows, width:])
        if image_far[at]:
            image_back[rows, 0:width] = image_sum.astype(BF16)
            image_back[rows, width:] = tails(loss_sum)
            iback_copies[at] = remote(
                block(image_back, at),
                block(image_got, at),
                iback_send.at[at],
                iback_recv.at[at],
                blk(0, -way * image_far[at], 0),
            )
    for at, copy in iback_copies.items():
        copy.wait_recv()
        rows = slice(at * size, (at + 1) * size)
        image_sum = image_sum + image_got[rows, :width].astype(F32)
        loss_sum = loss_sum + tail(image_got[rows, width:])
    image_out[...] = back(image_sum, image_unit, image_norm).astype(BF16)
    loss_sum = loss_sum / F32(len(reach) * len(text_far) * 2 * size)
    same = iota((size, size), 0) == iota((size, size), 1)
    loss_out[...] = jnp.sum(jnp.where(same, jnp.broadcast_to(loss_sum, (size, size)), 0.0), axis=0, keepdims=True)
    text_unit, text_norm = kept["text"]
    total = jnp.zeros((size, width), F32)
    for at, copy in back_copies.items():
        copy.wait_recv()
        total = total + text_got[at * size : (at + 1) * size, :].astype(F32)
    text_out[...] = back(total, text_unit, text_norm).astype(BF16)

    last = [core_copy] + list(side_copies.values()) + list(iback_copies.values()) + list(back_copies.values())
    for copy in row_copies + text_copies + image_copies + last:
        copy.wait_send()


def publish(image_ref, text_ref, loss_ref, image_out, text_out, loss_out, sems):
    copies = [
        pltpu.make_async_copy(src, dst, sems.at[at])
        for at, (src, dst) in enumerate(((image_ref, image_out), (text_ref, text_out), (loss_ref, loss_out)))
    ]
    for copy in copies:
        copy.start()
    for copy in copies:
        copy.wait()


def solution(mesh):
    depth = mesh.shape["blk"] // 4
    peers = mesh.shape["group"]
    image_far, text_far = offsets(depth)
    near = len(image_far)
    lines = len(text_far)

    def body(
        patches,
        patch_counts,
        dest_list,
        probe,
        w_attn_out,
        w_key,
        w_value,
        texts,
        image_labels,
        text_labels,
        log_temp,
        bias,
    ):
        rows, width = patches.shape
        size = texts.shape[0]
        padded = -(-rows // LANES) * LANES
        far = pl.BlockSpec(memory_space=pl.ANY)
        local = pl.BlockSpec(memory_space=pltpu.VMEM)
        dma = lambda n: pltpu.SemaphoreType.DMA((n,))
        image_grad, text_grad, row_loss = pl.pallas_call(
            functools.partial(kernel, depth, peers),
            out_shape=(
                pltpu.VMEM((size, width), BF16),
                pltpu.VMEM((size, width), BF16),
                pltpu.VMEM((1, size), F32),
            ),
            in_specs=[far] * 10 + [pl.BlockSpec(memory_space=pltpu.SMEM)] * 2,
            out_specs=(local, local, local),
            scratch_shapes=[
                pltpu.VMEM((1, peers), jnp.int32),
                pltpu.VMEM((1, peers), jnp.int32),
                pltpu.VMEM((width,), BF16),
                pltpu.VMEM((1, size), jnp.int32),
                pltpu.VMEM((1, size), jnp.int32),
                pltpu.VMEM((rows, width), BF16),
                pltpu.VMEM((width, width), BF16),
                pltpu.VMEM((width, width), BF16),
                pltpu.VMEM((width, width), BF16),
                pltpu.VMEM((size, width), BF16),
                pltpu.VMEM((padded, width), F32),
                pltpu.VMEM((peers, 1, width), F32),
                pltpu.VMEM((peers, 1, width), F32),
                pltpu.VMEM((size, width + LANES), BF16),
                pltpu.VMEM((2 * lines * size, width + LANES), BF16),
                pltpu.VMEM((2 * near * size, width + LANES), BF16),
                pltpu.VMEM((near * size, width + LANES), BF16),
                pltpu.VMEM((near * size, width + LANES), BF16),
                pltpu.VMEM((near * size, width + LANES), BF16),
                pltpu.VMEM((near * size, width + LANES), BF16),
                pltpu.VMEM((lines * size, width), BF16),
                pltpu.VMEM((lines * size, width), BF16),
                pltpu.VMEM((lines * size, width), BF16),
                pltpu.VMEM((lines * size, width), BF16),
                dma(7 + 3 * parts(width)),
                dma(peers),
                dma(peers),
                dma(lines + 1),
                dma(lines + 1),
                dma(2 * near),
                dma(2 * near),
                dma(near),
                dma(near),
                dma(lines),
                dma(lines),
                dma(1),
                dma(1),
                dma(near),
                dma(near),
            ],
            compiler_params=pltpu.CompilerParams(
                collective_id=0, has_side_effects=True, vmem_limit_bytes=62 * 1024 * 1024
            ),
            cost_estimate=pl.CostEstimate(
                flops=8 * rows * width * width, bytes_accessed=8 * width * width, transcendentals=0
            ),
            name="pool_and_contrast",
        )(
            patches,
            patch_counts,
            dest_list,
            probe,
            w_attn_out,
            w_key,
            w_value,
            texts,
            image_labels.reshape(1, size),
            text_labels.reshape(1, size),
            log_temp,
            bias,
        )
        image_grad, text_grad, row_loss = pl.pallas_call(
            publish,
            out_shape=(
                jax.ShapeDtypeStruct((size, width), BF16),
                jax.ShapeDtypeStruct((size, width), BF16),
                jax.ShapeDtypeStruct((1, size), F32),
            ),
            in_specs=[local] * 3,
            out_specs=(far, far, far),
            scratch_shapes=[dma(3)],
            name="publish",
        )(image_grad, text_grad, row_loss)
        return (image_grad, text_grad, row_loss.reshape(size))

    whole = P(("blk", "group"), None)
    flat = P(("blk", "group"))
    return jax.shard_map(
        body,
        mesh=mesh,
        in_specs=(whole, whole, whole, P(), P(), P(), P(), whole, flat, flat, P(), P()),
        out_specs=(whole, whole, flat),
        check_vma=False,
    )
```

```python
import functools

import jax
import jax.numpy as jnp
from jax import lax
from jax.experimental import pallas as pl
from jax.experimental.pallas import tpu as pltpu
from jax.sharding import PartitionSpec as P

HEADS = 16
LANES = 128
NEG = -1e30
F32 = jnp.float32
BF16 = jnp.bfloat16
NT = (((1,), (1,)), ((), ()))
TN = (((0,), (0,)), ((), ()))


def offsets(depth):
    if depth == 16:
        return ((0, 1, -1, 2), (-6, 6, -2, 2))
    if depth == 4:
        return ((0, 1), (-1, 1))
    raise ValueError("depth of z")


def parts(width):
    return 3 if width % (3 * LANES) == 0 else 1


def dot(a, b, dims=(((1,), (0,)), ((), ()))):
    return lax.dot_general(a, b, dims, preferred_element_type=F32)


def split(data, pieces):
    out = []
    for _ in range(pieces - 1):
        piece = data.astype(BF16)
        out.append(piece)
        data = data - piece.astype(F32)
    return out + [data.astype(BF16)]


def iota(shape, axis):
    return lax.broadcasted_iota(jnp.int32, shape, axis)


def column(row):
    n = row.shape[1]
    same = iota((n, n), 0) == iota((n, n), 1)
    return jnp.sum(jnp.where(same, jnp.broadcast_to(row, (n, n)), 0.0), axis=1, keepdims=True)


def unit(data):
    norm = jnp.sqrt(jnp.sum(data * data, axis=-1, keepdims=True) + 1e-06)
    return (data / norm, norm)


def back(grad, row_unit, norm):
    return (grad - row_unit * jnp.sum(row_unit * grad, axis=-1, keepdims=True)) / norm


def pool(patch, counts, dest, probe, key_w, proj_w, value_w, ready, normed):
    rows, width = patch.shape
    padded = normed.shape[0]
    head = width // HEADS
    images = counts.shape[1]
    cuts = parts(width)
    wide = width // cuts
    if padded > rows:
        normed[rows:padded, :] = jnp.zeros((padded - rows, width), F32)
    for cut in range(cuts):
        ready("proj", cut)
        normed[0:rows, cut * wide : (cut + 1) * wide] = dot(patch[...], proj_w[:, cut * wide : (cut + 1) * wide])
    proj = normed[0:rows, :]
    centre = proj - jnp.mean(proj, axis=-1, keepdims=True)
    normed[0:rows, :] = centre / jnp.sqrt(jnp.mean(centre * centre, axis=-1, keepdims=True) + 1e-06)
    low = iota((HEADS, width), 0) * head
    lane = iota((HEADS, width), 1)
    key_probe = []
    for cut in range(cuts):
        ready("key", cut)
        spread = jnp.where(
            (lane >= low) & (lane < low + head), jnp.broadcast_to(probe[...].astype(F32).reshape(1, width), (HEADS, width)), 0.0
        ).astype(BF16)
        key_probe.append(dot(spread, key_w[cut * wide : (cut + 1) * wide, :], NT))
    key_probe = jnp.concatenate(split(jnp.concatenate(key_probe, axis=1), 3), axis=0)
    pieces = split(normed[...], 2)
    scores = jnp.transpose(dot(pieces[1], key_probe, NT) + dot(pieces[0], key_probe, NT))
    scores = scores[:HEADS] + (scores[HEADS : 2 * HEADS] + scores[2 * HEADS : 3 * HEADS])
    scores = scores / jnp.sqrt(F32(head))
    image = iota((images, images), 0)
    which = iota((images, images), 1)
    lengths = jnp.broadcast_to(column(counts[...].astype(F32)), (images, images))
    first = jnp.sum(jnp.where(image < which, lengths, 0.0), axis=0, keepdims=True)
    last = jnp.sum(jnp.where(image <= which, lengths, 0.0), axis=0, keepdims=True)
    chosen = jnp.broadcast_to(dest[...], (images, images)) == image
    first = jnp.sum(jnp.where(chosen, jnp.broadcast_to(first, (images, images)), 0.0), axis=1, keepdims=True)
    last = jnp.sum(jnp.where(chosen, jnp.broadcast_to(last, (images, images)), 0.0), axis=1, keepdims=True)
    place = iota((images, padded), 1).astype(F32)
    member = ((place >= first) & (place < last))[None]
    masked = jnp.where(member, scores[:, None, :], NEG)
    expo = jnp.where(member, jnp.exp(masked - jnp.max(masked, axis=2, keepdims=True)), 0.0)
    weights = expo / jnp.sum(expo, axis=2, keepdims=True)
    weights = weights.reshape(HEADS * images, padded).astype(BF16)
    mixed = dot(weights, pieces[0]).astype(BF16)
    out = []
    for cut in range(cuts):
        ready("value", cut)
        first_head, last_head = cut * wide // head, -(-(cut + 1) * wide // head)
        taken = slice(first_head * images, last_head * images)
        full = dot(mixed[taken], value_w[:, cut * wide : (cut + 1) * wide])
        lane = iota((images, wide), 1) + cut * wide
        kept = jnp.zeros((images, wide), F32)
        for at in range(first_head, last_head):
            inside = (lane >= at * head) & (lane < at * head + head)
            kept = jnp.where(inside, full[(at - first_head) * images : (at - first_head + 1) * images], kept)
        out.append(kept)
    return jnp.concatenate(out, axis=1).astype(BF16).astype(F32)


def pairs(images, texts, width, temp, shift):
    logits = temp * dot(images[:, :width], texts[:, :width], NT) + shift
    apart = dot(images[:, width:], texts[:, width:], NT)
    signs = jnp.where(jnp.abs(apart) < 0.5, 1.0, -1.0).astype(F32)
    turned = -signs * logits
    small = jnp.exp(-jnp.abs(turned))
    loss = jnp.maximum(turned, 0.0) + jnp.log1p(small)
    sigmoid = jnp.where(turned >= 0, 1.0, small) / (1.0 + small)
    return (temp * -signs * sigmoid).astype(BF16), jnp.sum(loss, axis=1, keepdims=True)


def kernel(
    depth,
    peers,
    patches,
    counts_hbm,
    dest_hbm,
    probe_hbm,
    w_proj,
    w_key,
    w_value,
    texts,
    image_labels_hbm,
    text_labels_hbm,
    log_temp,
    bias,
    image_out,
    text_out,
    loss_out,
    counts,
    dest,
    probe,
    image_labels,
    text_labels,
    patch_buf,
    proj_buf,
    key_buf,
    value_buf,
    text_buf,
    normed,
    row_out,
    row_in,
    text_own,
    text_set,
    image_set,
    side_back,
    side_got,
    image_back,
    image_got,
    core_back,
    core_got,
    text_back,
    text_got,
    load_sem,
    row_send,
    row_recv,
    text_send,
    text_recv,
    image_send,
    image_recv,
    iback_send,
    iback_recv,
    tback_send,
    tback_recv,
    core_send,
    core_recv,
    side_send,
    side_recv,
):
    width = patches.shape[1]
    size = text_buf.shape[0]
    image_far, text_far = offsets(depth)
    reach = [(turn, far) for turn in (0, 1) for far in image_far]
    half = len(text_far) * size
    near = len(image_far)

    here = lax.axis_index("blk")
    mine = lax.axis_index("group")
    at_x, at_z, at_core = here // (2 * depth), (here // 2) % depth, here % 2
    way = 1 - 2 * at_core

    def blk(turn_x, far, turn_core):
        x = (at_x + turn_x) % 2
        z = (at_z + far + depth) % depth
        core = (at_core + turn_core) % 2
        return {"blk": (x * depth + z) * 2 + core}

    def remote(src, dst, send, recv, device):
        copy = pltpu.make_async_remote_copy(
            src_ref=src,
            dst_ref=dst,
            send_sem=send,
            recv_sem=recv,
            device_id=device,
            device_id_type=pl.DeviceIdType.MESH,
        )
        copy.start()
        return copy

    loads = {}

    def load(name, src, dst):
        loads[name] = pltpu.make_async_copy(src, dst, load_sem.at[len(loads)])
        loads[name].start()

    cuts = parts(width)
    wide = width // cuts
    load("patch", patches, patch_buf)
    for cut in range(cuts):
        some = pl.ds(cut * wide, wide)
        load(("proj", cut), w_proj.at[:, some], proj_buf.at[:, some])
    load("text", texts, text_buf)
    for name, src, dst in (
        ("counts", counts_hbm, counts),
        ("dest", dest_hbm, dest),
        ("probe", probe_hbm, probe),
        ("image_labels", image_labels_hbm, image_labels),
        ("text_labels", text_labels_hbm, text_labels),
    ):
        load(name, src, dst)
    for cut in range(cuts):
        some = pl.ds(cut * wide, wide)
        load(("key", cut), w_key.at[some, :], key_buf.at[some, :])
    for cut in range(cuts):
        some = pl.ds(cut * wide, wide)
        load(("value", cut), w_value.at[:, some], value_buf.at[:, some])

    known = {(turn, far % depth, 0) for turn, away in reach for far in (away, -away)}
    known |= {(0, far % depth, 0) for away in text_far for far in (away, -away)}
    known |= {(0, 0, 1)}
    known -= {(0, 0, 0)}
    barrier = pltpu.get_barrier_semaphore()
    for partner in sorted(known):
        pl.semaphore_signal(barrier, inc=1, device_id=blk(*partner), device_id_type=pl.DeviceIdType.MESH)
    for step in range(1, peers):
        pl.semaphore_signal(
            barrier, inc=1, device_id={"group": (mine + step) % peers}, device_id_type=pl.DeviceIdType.MESH
        )

    def block(ref, at, count=1):
        return ref.at[pl.ds(at * size, count * size), :]

    lane = iota((size, LANES), 1)
    loads["patch"].wait()
    text_copies = []
    kept = {}

    def ready(name, cut):
        loads[(name, cut)].wait()
        if name == "key" and cut == 0:
            for other in ("text", "counts", "dest", "probe", "image_labels", "text_labels"):
                loads[other].wait()
            text_unit, text_norm = unit(text_buf[...].astype(F32))
            kept["text"] = (text_unit, text_norm)
            text_own[:, 0:width] = text_unit.astype(BF16)
            text_label = column(text_labels[...].astype(F32))
            text_own[:, width:] = jnp.where(lane == 0, 1.0, jnp.where(lane == 1, -text_label, 0.0)).astype(BF16)

    ordered = pool(patch_buf, counts, dest, probe, key_buf, proj_buf, value_buf, ready, normed)
    for at in range(peers):
        row_out[at] = ordered[at : at + 1, :]
    pl.semaphore_wait(barrier, len(known) + peers - 1)
    row_copies = []
    for step in sorted(range(1, peers), key=lambda step: abs(step - peers // 2)):
        to = (mine + step) % peers
        row_copies.append(
            remote(
                row_out.at[to], row_in.at[mine], row_send.at[step], row_recv.at[step], {"group": to}
            )
        )
    row_in[mine] = row_out[mine]
    for at in range(len(text_far)):
        text_copies.append(
            remote(
                text_own,
                block(text_set, at),
                text_send.at[at],
                text_recv.at[at],
                blk(0, text_far[at], 0),
            )
        )

    for copy in row_copies:
        copy.wait_recv()
    placed = jnp.concatenate([row_in[at] for at in range(peers)], axis=0)
    image_unit, image_norm = unit(placed)
    image_set[0:size, 0:width] = image_unit.astype(BF16)
    image_label = column(image_labels[...].astype(F32))
    image_set[0:size, width:] = jnp.where(lane == 0, image_label, jnp.where(lane == 1, 1.0, 0.0)).astype(BF16)
    image_copies = []
    for at in sorted(range(1, len(reach)), key=lambda at: -abs(reach[at][1])):
        image_copies.append(
            remote(
                block(image_set, 0),
                block(image_set, at),
                image_send.at[at],
                image_recv.at[at],
                blk(reach[at][0], way * reach[at][1], 0),
            )
        )
    for copy in text_copies:
        copy.wait_recv()
    text_copies.append(
        remote(
            text_set.at[pl.ds(0, half), :],
            text_set.at[pl.ds(half, half), :],
            text_send.at[len(text_far)],
            text_recv.at[len(text_far)],
            blk(0, 0, 1),
        )
    )
    text_copies[-1].wait_recv()
    for copy in image_copies:
        copy.wait_recv()

    temp = jnp.exp(jnp.full((1, 1), log_temp[0], F32))
    weights, loss = pairs(image_set[...], text_set[...], width, temp, jnp.full((1, 1), bias[0], F32))
    text_part = dot(weights, image_set[:, :width], TN)
    core_back[...] = text_part[half:].astype(BF16)
    core_copy = remote(core_back, core_got, core_send.at[0], core_recv.at[0], blk(0, 0, 1))
    image_part = dot(weights, text_set[:, :width])

    def tails(data):
        wide_lane = iota((data.shape[0], LANES), 1)
        high, low = split(data, 2)
        return jnp.where(
            wide_lane == 0, high.astype(F32), jnp.where(wide_lane == 1, low.astype(F32), 0.0)
        ).astype(BF16)

    def tail(data):
        return jnp.sum(data.astype(F32), axis=1, keepdims=True)

    side_back[:, 0:width] = image_part[near * size :].astype(BF16)
    side_back[:, width:] = tails(loss[near * size :])
    order = sorted(range(near), key=lambda at: -abs(image_far[at]))
    side_copies = {}
    for at in order:
        side_copies[at] = remote(
            block(side_back, at), block(side_got, at), side_send.at[at], side_recv.at[at], blk(1, 0, 0)
        )
    core_copy.wait_recv()
    text_sum = text_part[:half] + core_got[...].astype(F32)
    text_back[...] = text_sum.astype(BF16)
    back_copies = {}
    for at in range(len(text_far)):
        back_copies[at] = remote(
            block(text_back, at),
            block(text_got, at),
            tback_send.at[at],
            tback_recv.at[at],
            blk(0, -text_far[at], 0),
        )
    iback_copies = {}
    for at in order:
        side_copies[at].wait_recv()
        rows = slice(at * size, (at + 1) * size)
        image_sum = image_part[rows] + side_got[rows, 0:width].astype(F32)
        loss_sum = loss[rows] + tail(side_got[rows, width:])
        if image_far[at]:
            image_back[rows, 0:width] = image_sum.astype(BF16)
            image_back[rows, width:] = tails(loss_sum)
            iback_copies[at] = remote(
                block(image_back, at),
                block(image_got, at),
                iback_send.at[at],
                iback_recv.at[at],
                blk(0, -way * image_far[at], 0),
            )
    for at, copy in iback_copies.items():
        copy.wait_recv()
        rows = slice(at * size, (at + 1) * size)
        image_sum = image_sum + image_got[rows, :width].astype(F32)
        loss_sum = loss_sum + tail(image_got[rows, width:])
    image_out[...] = back(image_sum, image_unit, image_norm).astype(BF16)
    loss_sum = loss_sum / F32(len(reach) * len(text_far) * 2 * size)
    same = iota((size, size), 0) == iota((size, size), 1)
    loss_out[...] = jnp.sum(jnp.where(same, jnp.broadcast_to(loss_sum, (size, size)), 0.0), axis=0, keepdims=True)
    text_unit, text_norm = kept["text"]
    total = jnp.zeros((size, width), F32)
    for at, copy in back_copies.items():
        copy.wait_recv()
        total = total + text_got[at * size : (at + 1) * size, :].astype(F32)
    text_out[...] = back(total, text_unit, text_norm).astype(BF16)

    last = [core_copy] + list(side_copies.values()) + list(iback_copies.values()) + list(back_copies.values())
    for copy in row_copies + text_copies + image_copies + last:
        copy.wait_send()


def solution(mesh):
    depth = mesh.shape["blk"] // 4
    peers = mesh.shape["group"]
    image_far, text_far = offsets(depth)
    near = len(image_far)
    lines = len(text_far)

    def body(
        patches,
        patch_counts,
        dest_list,
        probe,
        w_attn_out,
        w_key,
        w_value,
        texts,
        image_labels,
        text_labels,
        log_temp,
        bias,
    ):
        rows, width = patches.shape
        size = texts.shape[0]
        padded = -(-rows // LANES) * LANES
        far = pl.BlockSpec(memory_space=pl.ANY)
        local = pl.BlockSpec(memory_space=pltpu.VMEM)
        dma = lambda n: pltpu.SemaphoreType.DMA((n,))
        image_grad, text_grad, row_loss = pl.pallas_call(
            functools.partial(kernel, depth, peers),
            out_shape=(
                pltpu.VMEM((size, width), BF16),
                pltpu.VMEM((size, width), BF16),
                pltpu.VMEM((1, size), F32),
            ),
            in_specs=[far] * 10 + [pl.BlockSpec(memory_space=pltpu.SMEM)] * 2,
            out_specs=(local, local, local),
            scratch_shapes=[
                pltpu.VMEM((1, peers), jnp.int32),
                pltpu.VMEM((1, peers), jnp.int32),
                pltpu.VMEM((width,), BF16),
                pltpu.VMEM((1, size), jnp.int32),
                pltpu.VMEM((1, size), jnp.int32),
                pltpu.VMEM((rows, width), BF16),
                pltpu.VMEM((width, width), BF16),
                pltpu.VMEM((width, width), BF16),
                pltpu.VMEM((width, width), BF16),
                pltpu.VMEM((size, width), BF16),
                pltpu.VMEM((padded, width), F32),
                pltpu.VMEM((peers, 1, width), F32),
                pltpu.VMEM((peers, 1, width), F32),
                pltpu.VMEM((size, width + LANES), BF16),
                pltpu.VMEM((2 * lines * size, width + LANES), BF16),
                pltpu.VMEM((2 * near * size, width + LANES), BF16),
                pltpu.VMEM((near * size, width + LANES), BF16),
                pltpu.VMEM((near * size, width + LANES), BF16),
                pltpu.VMEM((near * size, width + LANES), BF16),
                pltpu.VMEM((near * size, width + LANES), BF16),
                pltpu.VMEM((lines * size, width), BF16),
                pltpu.VMEM((lines * size, width), BF16),
                pltpu.VMEM((lines * size, width), BF16),
                pltpu.VMEM((lines * size, width), BF16),
                dma(7 + 3 * parts(width)),
                dma(peers),
                dma(peers),
                dma(lines + 1),
                dma(lines + 1),
                dma(2 * near),
                dma(2 * near),
                dma(near),
                dma(near),
                dma(lines),
                dma(lines),
                dma(1),
                dma(1),
                dma(near),
                dma(near),
            ],
            compiler_params=pltpu.CompilerParams(
                collective_id=0, has_side_effects=True, vmem_limit_bytes=62 * 1024 * 1024
            ),
            cost_estimate=pl.CostEstimate(
                flops=8 * rows * width * width, bytes_accessed=8 * width * width, transcendentals=0
            ),
            name="pool_and_contrast",
        )(
            patches,
            patch_counts,
            dest_list,
            probe,
            w_attn_out,
            w_key,
            w_value,
            texts,
            image_labels.reshape(1, size),
            text_labels.reshape(1, size),
            log_temp,
            bias,
        )
        return (image_grad, text_grad, row_loss.reshape(size))

    whole = P(("blk", "group"), None)
    flat = P(("blk", "group"))
    return jax.shard_map(
        body,
        mesh=mesh,
        in_specs=(whole, whole, whole, P(), P(), P(), P(), whole, flat, flat, P(), P()),
        out_specs=(whole, whole, flat),
        check_vma=False,
    )
```

```python
import functools

import jax
import jax.numpy as jnp
from jax import lax
from jax.experimental import pallas as pl
from jax.experimental.pallas import tpu as pltpu
from jax.sharding import PartitionSpec as P

HEADS = 16
LANES = 128
NEG = -1e30
F32 = jnp.float32
BF16 = jnp.bfloat16
NT = (((1,), (1,)), ((), ()))
TN = (((0,), (0,)), ((), ()))


def offsets(depth):
    if depth == 16:
        return ((0, 1, -1, 2), (-6, 6, -2, 2))
    if depth == 4:
        return ((0, 1), (-1, 1))
    raise ValueError("depth of z")


def parts(width):
    return 3 if width % (3 * LANES) == 0 else 1


def dot(a, b, dims=(((1,), (0,)), ((), ()))):
    return lax.dot_general(a, b, dims, preferred_element_type=F32)


def split(data, pieces):
    out = []
    for _ in range(pieces - 1):
        piece = data.astype(BF16)
        out.append(piece)
        data = data - piece.astype(F32)
    return out + [data.astype(BF16)]


def iota(shape, axis):
    return lax.broadcasted_iota(jnp.int32, shape, axis)


def column(row):
    n = row.shape[1]
    same = iota((n, n), 0) == iota((n, n), 1)
    return jnp.sum(jnp.where(same, jnp.broadcast_to(row, (n, n)), 0.0), axis=1, keepdims=True)


def unit(data):
    norm = jnp.sqrt(jnp.sum(data * data, axis=-1, keepdims=True) + 1e-06)
    return (data / norm, norm)


def back(grad, row_unit, norm):
    return (grad - row_unit * jnp.sum(row_unit * grad, axis=-1, keepdims=True)) / norm


def pool(patch, counts, dest, probe, key_w, proj_w, value_w, ready, normed):
    rows, width = patch.shape
    padded = normed.shape[0]
    head = width // HEADS
    images = counts.shape[1]
    cuts = parts(width)
    wide = width // cuts
    if padded > rows:
        normed[rows:padded, :] = jnp.zeros((padded - rows, width), F32)
    for cut in range(cuts):
        ready("proj", cut)
        normed[0:rows, cut * wide : (cut + 1) * wide] = dot(patch[...], proj_w[:, cut * wide : (cut + 1) * wide])
    proj = normed[0:rows, :]
    centre = proj - jnp.mean(proj, axis=-1, keepdims=True)
    normed[0:rows, :] = centre / jnp.sqrt(jnp.mean(centre * centre, axis=-1, keepdims=True) + 1e-06)
    low = iota((HEADS, width), 0) * head
    lane = iota((HEADS, width), 1)
    key_probe = []
    for cut in range(cuts):
        ready("key", cut)
        spread = jnp.where(
            (lane >= low) & (lane < low + head), jnp.broadcast_to(probe[...].astype(F32).reshape(1, width), (HEADS, width)), 0.0
        ).astype(BF16)
        key_probe.append(dot(spread, key_w[cut * wide : (cut + 1) * wide, :], NT))
    key_probe = jnp.concatenate(split(jnp.concatenate(key_probe, axis=1), 3), axis=0)
    pieces = split(normed[...], 2)
    scores = jnp.transpose(dot(pieces[1], key_probe, NT) + dot(pieces[0], key_probe, NT))
    scores = scores[:HEADS] + (scores[HEADS : 2 * HEADS] + scores[2 * HEADS : 3 * HEADS])
    scores = scores / jnp.sqrt(F32(head))
    image = iota((images, images), 0)
    which = iota((images, images), 1)
    lengths = jnp.broadcast_to(column(counts[...].astype(F32)), (images, images))
    first = jnp.sum(jnp.where(image < which, lengths, 0.0), axis=0, keepdims=True)
    last = jnp.sum(jnp.where(image <= which, lengths, 0.0), axis=0, keepdims=True)
    chosen = jnp.broadcast_to(dest[...], (images, images)) == image
    first = jnp.sum(jnp.where(chosen, jnp.broadcast_to(first, (images, images)), 0.0), axis=1, keepdims=True)
    last = jnp.sum(jnp.where(chosen, jnp.broadcast_to(last, (images, images)), 0.0), axis=1, keepdims=True)
    place = iota((images, padded), 1).astype(F32)
    member = ((place >= first) & (place < last))[None]
    masked = jnp.where(member, scores[:, None, :], NEG)
    expo = jnp.where(member, jnp.exp(masked - jnp.max(masked, axis=2, keepdims=True)), 0.0)
    weights = expo / jnp.sum(expo, axis=2, keepdims=True)
    weights = weights.reshape(HEADS * images, padded).astype(BF16)
    mixed = dot(weights, pieces[0]).astype(BF16)
    out = []
    for cut in range(cuts):
        ready("value", cut)
        first_head, last_head = cut * wide // head, -(-(cut + 1) * wide // head)
        taken = slice(first_head * images, last_head * images)
        full = dot(mixed[taken], value_w[:, cut * wide : (cut + 1) * wide])
        lane = iota((images, wide), 1) + cut * wide
        kept = jnp.zeros((images, wide), F32)
        for at in range(first_head, last_head):
            inside = (lane >= at * head) & (lane < at * head + head)
            kept = jnp.where(inside, full[(at - first_head) * images : (at - first_head + 1) * images], kept)
        out.append(kept)
    return jnp.concatenate(out, axis=1).astype(BF16).astype(F32)


def pairs(images, texts, width, temp, shift):
    logits = temp * dot(images[:, :width], texts[:, :width], NT) + shift
    apart = dot(images[:, width:], texts[:, width:], NT)
    signs = jnp.where(jnp.abs(apart) < 0.5, 1.0, -1.0).astype(F32)
    turned = -signs * logits
    small = jnp.exp(-jnp.abs(turned))
    loss = jnp.maximum(turned, 0.0) + jnp.log1p(small)
    sigmoid = jnp.where(turned >= 0, 1.0, small) / (1.0 + small)
    return (temp * -signs * sigmoid).astype(BF16), jnp.sum(loss, axis=1, keepdims=True)


def kernel(
    depth,
    peers,
    patches,
    counts_hbm,
    dest_hbm,
    probe_hbm,
    w_proj,
    w_key,
    w_value,
    texts,
    image_labels_hbm,
    text_labels_hbm,
    log_temp,
    bias,
    image_out,
    text_out,
    loss_out,
    counts,
    dest,
    probe,
    image_labels,
    text_labels,
    patch_buf,
    proj_buf,
    key_buf,
    value_buf,
    text_buf,
    normed,
    row_out,
    row_in,
    text_own,
    text_set,
    image_set,
    side_back,
    side_got,
    image_back,
    image_got,
    core_back,
    core_got,
    text_back,
    text_got,
    load_sem,
    row_send,
    row_recv,
    text_send,
    text_recv,
    image_send,
    image_recv,
    iback_send,
    iback_recv,
    tback_send,
    tback_recv,
    core_send,
    core_recv,
    side_send,
    side_recv,
):
    width = patches.shape[1]
    size = text_buf.shape[0]
    image_far, text_far = offsets(depth)
    reach = [(turn, far) for turn in (0, 1) for far in image_far]
    half = len(text_far) * size
    near = len(image_far)

    here = lax.axis_index("blk")
    mine = lax.axis_index("group")
    at_x, at_z, at_core = here // (2 * depth), (here // 2) % depth, here % 2
    way = 1 - 2 * at_core

    def blk(turn_x, far, turn_core):
        x = (at_x + turn_x) % 2
        z = (at_z + far + depth) % depth
        core = (at_core + turn_core) % 2
        return {"blk": (x * depth + z) * 2 + core}

    def remote(src, dst, send, recv, device):
        copy = pltpu.make_async_remote_copy(
            src_ref=src,
            dst_ref=dst,
            send_sem=send,
            recv_sem=recv,
            device_id=device,
            device_id_type=pl.DeviceIdType.MESH,
        )
        copy.start()
        return copy

    loads = {}

    def load(name, src, dst):
        loads[name] = pltpu.make_async_copy(src, dst, load_sem.at[len(loads)])
        loads[name].start()

    cuts = parts(width)
    wide = width // cuts
    load("patch", patches, patch_buf)
    for cut in range(cuts):
        some = pl.ds(cut * wide, wide)
        load(("proj", cut), w_proj.at[:, some], proj_buf.at[:, some])
    load("text", texts, text_buf)
    for name, src, dst in (
        ("counts", counts_hbm, counts),
        ("dest", dest_hbm, dest),
        ("probe", probe_hbm, probe),
        ("image_labels", image_labels_hbm, image_labels),
        ("text_labels", text_labels_hbm, text_labels),
    ):
        load(name, src, dst)
    for cut in range(cuts):
        some = pl.ds(cut * wide, wide)
        load(("key", cut), w_key.at[some, :], key_buf.at[some, :])
    for cut in range(cuts):
        some = pl.ds(cut * wide, wide)
        load(("value", cut), w_value.at[:, some], value_buf.at[:, some])

    known = {(turn, far % depth, 0) for turn, away in reach for far in (away, -away)}
    known |= {(0, far % depth, 0) for away in text_far for far in (away, -away)}
    known |= {(0, 0, 1)}
    known -= {(0, 0, 0)}
    barrier = pltpu.get_barrier_semaphore()
    for partner in sorted(known):
        pl.semaphore_signal(barrier, inc=1, device_id=blk(*partner), device_id_type=pl.DeviceIdType.MESH)
    for step in range(1, peers):
        pl.semaphore_signal(
            barrier, inc=1, device_id={"group": (mine + step) % peers}, device_id_type=pl.DeviceIdType.MESH
        )

    def block(ref, at, count=1):
        return ref.at[pl.ds(at * size, count * size), :]

    lane = iota((size, LANES), 1)
    loads["patch"].wait()
    text_copies = []
    kept = {}

    def ready(name, cut):
        loads[(name, cut)].wait()
        if name == "key" and cut == 0:
            for other in ("text", "counts", "dest", "probe", "image_labels", "text_labels"):
                loads[other].wait()
            text_unit, text_norm = unit(text_buf[...].astype(F32))
            kept["text"] = (text_unit, text_norm)
            text_own[:, 0:width] = text_unit.astype(BF16)
            text_label = column(text_labels[...].astype(F32))
            text_own[:, width:] = jnp.where(lane == 0, 1.0, jnp.where(lane == 1, -text_label, 0.0)).astype(BF16)
        if name == "value" and cut == 0:
            pl.semaphore_wait(barrier, len(known) + peers - 1)
            for at in range(len(text_far)):
                text_copies.append(
                    remote(
                        text_own,
                        block(text_set, at),
                        text_send.at[at],
                        text_recv.at[at],
                        blk(0, text_far[at], 0),
                    )
                )

    ordered = pool(patch_buf, counts, dest, probe, key_buf, proj_buf, value_buf, ready, normed)
    for at in range(peers):
        row_out[at] = ordered[at : at + 1, :]
    row_copies = []
    for step in sorted(range(1, peers), key=lambda step: abs(step - peers // 2)):
        to = (mine + step) % peers
        row_copies.append(
            remote(
                row_out.at[to], row_in.at[mine], row_send.at[step], row_recv.at[step], {"group": to}
            )
        )
    row_in[mine] = row_out[mine]
    for copy in row_copies:
        copy.wait_recv()
    placed = jnp.concatenate([row_in[at] for at in range(peers)], axis=0)
    image_unit, image_norm = unit(placed)
    image_set[0:size, 0:width] = image_unit.astype(BF16)
    image_label = column(image_labels[...].astype(F32))
    image_set[0:size, width:] = jnp.where(lane == 0, image_label, jnp.where(lane == 1, 1.0, 0.0)).astype(BF16)
    image_copies = []
    for at in sorted(range(1, len(reach)), key=lambda at: -abs(reach[at][1])):
        image_copies.append(
            remote(
                block(image_set, 0),
                block(image_set, at),
                image_send.at[at],
                image_recv.at[at],
                blk(reach[at][0], way * reach[at][1], 0),
            )
        )
    for copy in text_copies:
        copy.wait_recv()
    text_copies.append(
        remote(
            text_set.at[pl.ds(0, half), :],
            text_set.at[pl.ds(half, half), :],
            text_send.at[len(text_far)],
            text_recv.at[len(text_far)],
            blk(0, 0, 1),
        )
    )
    text_copies[-1].wait_recv()
    for copy in image_copies:
        copy.wait_recv()

    temp = jnp.exp(jnp.full((1, 1), log_temp[0], F32))
    weights, loss = pairs(image_set[...], text_set[...], width, temp, jnp.full((1, 1), bias[0], F32))
    text_part = dot(weights, image_set[:, :width], TN)
    core_back[...] = text_part[half:].astype(BF16)
    core_copies = [
        remote(block(core_back, at), block(core_got, at), core_send.at[at], core_recv.at[at], blk(0, 0, 1))
        for at in range(len(text_far))
    ]
    image_part = dot(weights, text_set[:, :width])

    def tails(data):
        wide_lane = iota((data.shape[0], LANES), 1)
        high, low = split(data, 2)
        return jnp.where(
            wide_lane == 0, high.astype(F32), jnp.where(wide_lane == 1, low.astype(F32), 0.0)
        ).astype(BF16)

    def tail(data):
        return jnp.sum(data.astype(F32), axis=1, keepdims=True)

    side_back[:, 0:width] = image_part[near * size :].astype(BF16)
    side_back[:, width:] = tails(loss[near * size :])
    order = sorted(range(near), key=lambda at: -abs(image_far[at]))
    side_copies = {}
    for at in order:
        side_copies[at] = remote(
            block(side_back, at), block(side_got, at), side_send.at[at], side_recv.at[at], blk(1, 0, 0)
        )
    back_copies = {}
    for at in range(len(text_far)):
        core_copies[at].wait_recv()
        rows = slice(at * size, (at + 1) * size)
        text_back[rows, :] = (text_part[rows] + core_got[rows, :].astype(F32)).astype(BF16)
        back_copies[at] = remote(
            block(text_back, at),
            block(text_got, at),
            tback_send.at[at],
            tback_recv.at[at],
            blk(0, -text_far[at], 0),
        )
    iback_copies = {}
    for at in order:
        side_copies[at].wait_recv()
        rows = slice(at * size, (at + 1) * size)
        image_sum = image_part[rows] + side_got[rows, 0:width].astype(F32)
        loss_sum = loss[rows] + tail(side_got[rows, width:])
        if image_far[at]:
            image_back[rows, 0:width] = image_sum.astype(BF16)
            image_back[rows, width:] = tails(loss_sum)
            iback_copies[at] = remote(
                block(image_back, at),
                block(image_got, at),
                iback_send.at[at],
                iback_recv.at[at],
                blk(0, -way * image_far[at], 0),
            )
    for at, copy in iback_copies.items():
        copy.wait_recv()
        rows = slice(at * size, (at + 1) * size)
        image_sum = image_sum + image_got[rows, :width].astype(F32)
        loss_sum = loss_sum + tail(image_got[rows, width:])
    image_out[...] = back(image_sum, image_unit, image_norm).astype(BF16)
    loss_sum = loss_sum / F32(len(reach) * len(text_far) * 2 * size)
    same = iota((size, size), 0) == iota((size, size), 1)
    loss_out[...] = jnp.sum(jnp.where(same, jnp.broadcast_to(loss_sum, (size, size)), 0.0), axis=0, keepdims=True)
    text_unit, text_norm = kept["text"]
    total = jnp.zeros((size, width), F32)
    for at, copy in back_copies.items():
        copy.wait_recv()
        total = total + text_got[at * size : (at + 1) * size, :].astype(F32)
    text_out[...] = back(total, text_unit, text_norm).astype(BF16)

    last = core_copies + list(side_copies.values()) + list(iback_copies.values()) + list(back_copies.values())
    for copy in row_copies + text_copies + image_copies + last:
        copy.wait_send()


def solution(mesh):
    depth = mesh.shape["blk"] // 4
    peers = mesh.shape["group"]
    image_far, text_far = offsets(depth)
    near = len(image_far)
    lines = len(text_far)

    def body(
        patches,
        patch_counts,
        dest_list,
        probe,
        w_attn_out,
        w_key,
        w_value,
        texts,
        image_labels,
        text_labels,
        log_temp,
        bias,
    ):
        rows, width = patches.shape
        size = texts.shape[0]
        padded = -(-rows // LANES) * LANES
        far = pl.BlockSpec(memory_space=pl.ANY)
        local = pl.BlockSpec(memory_space=pltpu.VMEM)
        dma = lambda n: pltpu.SemaphoreType.DMA((n,))
        image_grad, text_grad, row_loss = pl.pallas_call(
            functools.partial(kernel, depth, peers),
            out_shape=(
                pltpu.VMEM((size, width), BF16),
                pltpu.VMEM((size, width), BF16),
                pltpu.VMEM((1, size), F32),
            ),
            in_specs=[far] * 10 + [pl.BlockSpec(memory_space=pltpu.SMEM)] * 2,
            out_specs=(local, local, local),
            scratch_shapes=[
                pltpu.VMEM((1, peers), jnp.int32),
                pltpu.VMEM((1, peers), jnp.int32),
                pltpu.VMEM((width,), BF16),
                pltpu.VMEM((1, size), jnp.int32),
                pltpu.VMEM((1, size), jnp.int32),
                pltpu.VMEM((rows, width), BF16),
                pltpu.VMEM((width, width), BF16),
                pltpu.VMEM((width, width), BF16),
                pltpu.VMEM((width, width), BF16),
                pltpu.VMEM((size, width), BF16),
                pltpu.VMEM((padded, width), F32),
                pltpu.VMEM((peers, 1, width), F32),
                pltpu.VMEM((peers, 1, width), F32),
                pltpu.VMEM((size, width + LANES), BF16),
                pltpu.VMEM((2 * lines * size, width + LANES), BF16),
                pltpu.VMEM((2 * near * size, width + LANES), BF16),
                pltpu.VMEM((near * size, width + LANES), BF16),
                pltpu.VMEM((near * size, width + LANES), BF16),
                pltpu.VMEM((near * size, width + LANES), BF16),
                pltpu.VMEM((near * size, width + LANES), BF16),
                pltpu.VMEM((lines * size, width), BF16),
                pltpu.VMEM((lines * size, width), BF16),
                pltpu.VMEM((lines * size, width), BF16),
                pltpu.VMEM((lines * size, width), BF16),
                dma(7 + 3 * parts(width)),
                dma(peers),
                dma(peers),
                dma(lines + 1),
                dma(lines + 1),
                dma(2 * near),
                dma(2 * near),
                dma(near),
                dma(near),
                dma(lines),
                dma(lines),
                dma(lines),
                dma(lines),
                dma(near),
                dma(near),
            ],
            compiler_params=pltpu.CompilerParams(
                collective_id=0, has_side_effects=True, vmem_limit_bytes=62 * 1024 * 1024
            ),
            cost_estimate=pl.CostEstimate(
                flops=8 * rows * width * width, bytes_accessed=8 * width * width, transcendentals=0
            ),
            name="pool_and_contrast",
        )(
            patches,
            patch_counts,
            dest_list,
            probe,
            w_attn_out,
            w_key,
            w_value,
            texts,
            image_labels.reshape(1, size),
            text_labels.reshape(1, size),
            log_temp,
            bias,
        )
        return (image_grad, text_grad, row_loss.reshape(size))

    whole = P(("blk", "group"), None)
    flat = P(("blk", "group"))
    return jax.shard_map(
        body,
        mesh=mesh,
        in_specs=(whole, whole, whole, P(), P(), P(), P(), whole, flat, flat, P(), P()),
        out_specs=(whole, whole, flat),
        check_vma=False,
    )
```

```python
import functools

import jax
import jax.numpy as jnp
from jax import lax
from jax.experimental import pallas as pl
from jax.experimental.pallas import tpu as pltpu
from jax.sharding import PartitionSpec as P

HEADS = 16
LANES = 128
NEG = -1e30
F32 = jnp.float32
BF16 = jnp.bfloat16
NT = (((1,), (1,)), ((), ()))
TN = (((0,), (0,)), ((), ()))


def offsets(depth):
    if depth == 16:
        return ((0, 1, -1, 2), (-6, 6, -2, 2))
    if depth == 4:
        return ((0, 1), (-1, 1))
    raise ValueError("depth of z")


def parts(width):
    return 3 if width % (3 * LANES) == 0 else 1


def dot(a, b, dims=(((1,), (0,)), ((), ()))):
    return lax.dot_general(a, b, dims, preferred_element_type=F32)


def split(data, pieces):
    out = []
    for _ in range(pieces - 1):
        piece = data.astype(BF16)
        out.append(piece)
        data = data - piece.astype(F32)
    return out + [data.astype(BF16)]


def iota(shape, axis):
    return lax.broadcasted_iota(jnp.int32, shape, axis)


def column(row):
    n = row.shape[1]
    same = iota((n, n), 0) == iota((n, n), 1)
    return jnp.sum(jnp.where(same, jnp.broadcast_to(row, (n, n)), 0.0), axis=1, keepdims=True)


def unit(data):
    norm = jnp.sqrt(jnp.sum(data * data, axis=-1, keepdims=True) + 1e-06)
    return (data / norm, norm)


def back(grad, row_unit, norm):
    return (grad - row_unit * jnp.sum(row_unit * grad, axis=-1, keepdims=True)) / norm


def pool(patch, counts, dest, probe, key_w, proj_w, value_w, ready, normed):
    rows, width = patch.shape
    padded = normed.shape[0]
    head = width // HEADS
    images = counts.shape[1]
    cuts = parts(width)
    wide = width // cuts
    if padded > rows:
        normed[rows:padded, :] = jnp.zeros((padded - rows, width), F32)
    for cut in range(cuts):
        ready("proj", cut)
        normed[0:rows, cut * wide : (cut + 1) * wide] = dot(patch[...], proj_w[:, cut * wide : (cut + 1) * wide])
    proj = normed[0:rows, :]
    centre = proj - jnp.mean(proj, axis=-1, keepdims=True)
    normed[0:rows, :] = centre / jnp.sqrt(jnp.mean(centre * centre, axis=-1, keepdims=True) + 1e-06)
    low = iota((HEADS, width), 0) * head
    lane = iota((HEADS, width), 1)
    key_probe = []
    for cut in range(cuts):
        ready("key", cut)
        spread = jnp.where(
            (lane >= low) & (lane < low + head), jnp.broadcast_to(probe[...].astype(F32).reshape(1, width), (HEADS, width)), 0.0
        ).astype(BF16)
        key_probe.append(dot(spread, key_w[cut * wide : (cut + 1) * wide, :], NT))
    key_probe = jnp.concatenate(split(jnp.concatenate(key_probe, axis=1), 3), axis=0)
    pieces = split(normed[...], 2)
    scores = jnp.transpose(dot(pieces[1], key_probe, NT) + dot(pieces[0], key_probe, NT))
    scores = scores[:HEADS] + (scores[HEADS : 2 * HEADS] + scores[2 * HEADS : 3 * HEADS])
    scores = scores / jnp.sqrt(F32(head))
    image = iota((images, images), 0)
    which = iota((images, images), 1)
    lengths = jnp.broadcast_to(column(counts[...].astype(F32)), (images, images))
    first = jnp.sum(jnp.where(image < which, lengths, 0.0), axis=0, keepdims=True)
    last = jnp.sum(jnp.where(image <= which, lengths, 0.0), axis=0, keepdims=True)
    chosen = jnp.broadcast_to(dest[...], (images, images)) == image
    first = jnp.sum(jnp.where(chosen, jnp.broadcast_to(first, (images, images)), 0.0), axis=1, keepdims=True)
    last = jnp.sum(jnp.where(chosen, jnp.broadcast_to(last, (images, images)), 0.0), axis=1, keepdims=True)
    place = iota((images, padded), 1).astype(F32)
    member = ((place >= first) & (place < last))[None]
    masked = jnp.where(member, scores[:, None, :], NEG)
    expo = jnp.where(member, jnp.exp(masked - jnp.max(masked, axis=2, keepdims=True)), 0.0)
    weights = expo / jnp.sum(expo, axis=2, keepdims=True)
    weights = weights.reshape(HEADS * images, padded).astype(BF16)
    mixed = dot(weights, pieces[0]).astype(BF16)
    out = []
    for cut in range(cuts):
        ready("value", cut)
        first_head, last_head = cut * wide // head, -(-(cut + 1) * wide // head)
        taken = slice(first_head * images, last_head * images)
        full = dot(mixed[taken], value_w[:, cut * wide : (cut + 1) * wide])
        lane = iota((images, wide), 1) + cut * wide
        kept = jnp.zeros((images, wide), F32)
        for at in range(first_head, last_head):
            inside = (lane >= at * head) & (lane < at * head + head)
            kept = jnp.where(inside, full[(at - first_head) * images : (at - first_head + 1) * images], kept)
        out.append(kept)
    return jnp.concatenate(out, axis=1).astype(BF16).astype(F32)


def pairs(images, texts, width, temp, shift):
    logits = temp * dot(images[:, :width], texts[:, :width], NT) + shift
    apart = dot(images[:, width:], texts[:, width:], NT)
    signs = jnp.where(jnp.abs(apart) < 0.5, 1.0, -1.0).astype(F32)
    turned = -signs * logits
    small = jnp.exp(-jnp.abs(turned))
    loss = jnp.maximum(turned, 0.0) + jnp.log1p(small)
    sigmoid = jnp.where(turned >= 0, 1.0, small) / (1.0 + small)
    return (temp * -signs * sigmoid).astype(BF16), jnp.sum(loss, axis=1, keepdims=True)


def kernel(
    depth,
    peers,
    patches,
    counts_hbm,
    dest_hbm,
    probe_hbm,
    w_proj,
    w_key,
    w_value,
    texts,
    image_labels_hbm,
    text_labels_hbm,
    log_temp,
    bias,
    image_out,
    text_out,
    loss_out,
    counts,
    dest,
    probe,
    image_labels,
    text_labels,
    patch_buf,
    proj_buf,
    key_buf,
    value_buf,
    text_buf,
    normed,
    row_out,
    row_in,
    text_own,
    text_set,
    image_set,
    side_back,
    side_got,
    image_back,
    image_got,
    core_back,
    core_got,
    text_back,
    text_got,
    load_sem,
    row_send,
    row_recv,
    text_send,
    text_recv,
    image_send,
    image_recv,
    iback_send,
    iback_recv,
    tback_send,
    tback_recv,
    core_send,
    core_recv,
    side_send,
    side_recv,
):
    width = patches.shape[1]
    size = text_buf.shape[0]
    image_far, text_far = offsets(depth)
    reach = [(turn, far) for turn in (0, 1) for far in image_far]
    half = len(text_far) * size
    near = len(image_far)

    here = lax.axis_index("blk")
    mine = lax.axis_index("group")
    at_x, at_z, at_core = here // (2 * depth), (here // 2) % depth, here % 2
    way = 1 - 2 * at_core

    def blk(turn_x, far, turn_core):
        x = (at_x + turn_x) % 2
        z = (at_z + far + depth) % depth
        core = (at_core + turn_core) % 2
        return {"blk": (x * depth + z) * 2 + core}

    def remote(src, dst, send, recv, device):
        copy = pltpu.make_async_remote_copy(
            src_ref=src,
            dst_ref=dst,
            send_sem=send,
            recv_sem=recv,
            device_id=device,
            device_id_type=pl.DeviceIdType.MESH,
        )
        copy.start()
        return copy

    loads = {}

    def load(name, src, dst):
        loads[name] = pltpu.make_async_copy(src, dst, load_sem.at[len(loads)])
        loads[name].start()

    cuts = parts(width)
    wide = width // cuts
    load("patch", patches, patch_buf)
    for cut in range(cuts):
        some = pl.ds(cut * wide, wide)
        load(("proj", cut), w_proj.at[:, some], proj_buf.at[:, some])
    load("text", texts, text_buf)
    for name, src, dst in (
        ("counts", counts_hbm, counts),
        ("dest", dest_hbm, dest),
        ("probe", probe_hbm, probe),
        ("image_labels", image_labels_hbm, image_labels),
        ("text_labels", text_labels_hbm, text_labels),
    ):
        load(name, src, dst)
    for cut in range(cuts):
        some = pl.ds(cut * wide, wide)
        load(("key", cut), w_key.at[some, :], key_buf.at[some, :])
    for cut in range(cuts):
        some = pl.ds(cut * wide, wide)
        load(("value", cut), w_value.at[:, some], value_buf.at[:, some])

    known = {(turn, far % depth, 0) for turn, away in reach for far in (away, -away)}
    known |= {(0, far % depth, 0) for away in text_far for far in (away, -away)}
    known |= {(0, 0, 1)}
    known -= {(0, 0, 0)}
    barrier = pltpu.get_barrier_semaphore()
    for partner in sorted(known):
        pl.semaphore_signal(barrier, inc=1, device_id=blk(*partner), device_id_type=pl.DeviceIdType.MESH)
    for step in range(1, peers):
        pl.semaphore_signal(
            barrier, inc=1, device_id={"group": (mine + step) % peers}, device_id_type=pl.DeviceIdType.MESH
        )

    def block(ref, at, count=1):
        return ref.at[pl.ds(at * size, count * size), :]

    lane = iota((size, LANES), 1)
    loads["patch"].wait()
    text_copies = []
    kept = {}

    def ready(name, cut):
        loads[(name, cut)].wait()
        if name == "key" and cut == 0:
            for other in ("text", "counts", "dest", "probe", "image_labels", "text_labels"):
                loads[other].wait()
            text_unit, text_norm = unit(text_buf[...].astype(F32))
            kept["text"] = (text_unit, text_norm)
            text_own[:, 0:width] = text_unit.astype(BF16)
            text_label = column(text_labels[...].astype(F32))
            text_own[:, width:] = jnp.where(lane == 0, 1.0, jnp.where(lane == 1, -text_label, 0.0)).astype(BF16)
        if name == "value" and cut == 0:
            pl.semaphore_wait(barrier, len(known) + peers - 1)
            for at in range(len(text_far)):
                text_copies.append(
                    remote(
                        text_own,
                        block(text_set, at),
                        text_send.at[at],
                        text_recv.at[at],
                        blk(0, text_far[at], 0),
                    )
                )

    ordered = pool(patch_buf, counts, dest, probe, key_buf, proj_buf, value_buf, ready, normed)
    for at in range(peers):
        row_out[at] = ordered[at : at + 1, :]
    row_copies = []
    for step in sorted(range(1, peers), key=lambda step: abs(step - peers // 2)):
        to = (mine + step) % peers
        row_copies.append(
            remote(
                row_out.at[to], row_in.at[mine], row_send.at[step], row_recv.at[step], {"group": to}
            )
        )
    row_in[mine] = row_out[mine]
    image_label = column(image_labels[...].astype(F32))
    image_set[0:size, width:] = jnp.where(lane == 0, image_label, jnp.where(lane == 1, 1.0, 0.0)).astype(BF16)
    temp = jnp.exp(jnp.full((1, 1), log_temp[0], F32))
    for copy in row_copies:
        copy.wait_recv()
    placed = jnp.concatenate([row_in[at] for at in range(peers)], axis=0)
    image_unit, image_norm = unit(placed)
    image_set[0:size, 0:width] = image_unit.astype(BF16)
    image_copies = []
    for at in sorted(range(1, len(reach)), key=lambda at: -abs(reach[at][1])):
        image_copies.append(
            remote(
                block(image_set, 0),
                block(image_set, at),
                image_send.at[at],
                image_recv.at[at],
                blk(reach[at][0], way * reach[at][1], 0),
            )
        )
    for copy in text_copies:
        copy.wait_recv()
    text_copies.append(
        remote(
            text_set.at[pl.ds(0, half), :],
            text_set.at[pl.ds(half, half), :],
            text_send.at[len(text_far)],
            text_recv.at[len(text_far)],
            blk(0, 0, 1),
        )
    )
    text_copies[-1].wait_recv()
    for copy in image_copies:
        copy.wait_recv()

    weights, loss = pairs(image_set[...], text_set[...], width, temp, jnp.full((1, 1), bias[0], F32))
    core_back[...] = dot(weights[:, half:], image_set[:, :width], TN).astype(BF16)
    core_copies = [
        remote(block(core_back, at), block(core_got, at), core_send.at[at], core_recv.at[at], blk(0, 0, 1))
        for at in range(len(text_far))
    ]

    def tails(data):
        wide_lane = iota((data.shape[0], LANES), 1)
        high, low = split(data, 2)
        return jnp.where(
            wide_lane == 0, high.astype(F32), jnp.where(wide_lane == 1, low.astype(F32), 0.0)
        ).astype(BF16)

    def tail(data):
        return jnp.sum(data.astype(F32), axis=1, keepdims=True)

    side_back[:, 0:width] = dot(weights[near * size :], text_set[:, :width]).astype(BF16)
    side_back[:, width:] = tails(loss[near * size :])
    order = sorted(range(near), key=lambda at: -abs(image_far[at]))
    side_copies = {}
    for at in order:
        side_copies[at] = remote(
            block(side_back, at), block(side_got, at), side_send.at[at], side_recv.at[at], blk(1, 0, 0)
        )
    text_part = dot(weights[:, :half], image_set[:, :width], TN)
    image_part = dot(weights[: near * size], text_set[:, :width])
    back_copies = {}
    for at in range(len(text_far)):
        core_copies[at].wait_recv()
        rows = slice(at * size, (at + 1) * size)
        text_back[rows, :] = (text_part[rows] + core_got[rows, :].astype(F32)).astype(BF16)
        back_copies[at] = remote(
            block(text_back, at),
            block(text_got, at),
            tback_send.at[at],
            tback_recv.at[at],
            blk(0, -text_far[at], 0),
        )
    iback_copies = {}
    for at in order:
        side_copies[at].wait_recv()
        rows = slice(at * size, (at + 1) * size)
        image_sum = image_part[rows] + side_got[rows, 0:width].astype(F32)
        loss_sum = loss[rows] + tail(side_got[rows, width:])
        if image_far[at]:
            image_back[rows, 0:width] = image_sum.astype(BF16)
            image_back[rows, width:] = tails(loss_sum)
            iback_copies[at] = remote(
                block(image_back, at),
                block(image_got, at),
                iback_send.at[at],
                iback_recv.at[at],
                blk(0, -way * image_far[at], 0),
            )
    for at, copy in iback_copies.items():
        copy.wait_recv()
        rows = slice(at * size, (at + 1) * size)
        image_sum = image_sum + image_got[rows, :width].astype(F32)
        loss_sum = loss_sum + tail(image_got[rows, width:])
    image_out[...] = back(image_sum, image_unit, image_norm).astype(BF16)
    loss_sum = loss_sum / F32(len(reach) * len(text_far) * 2 * size)
    same = iota((size, size), 0) == iota((size, size), 1)
    loss_out[...] = jnp.sum(jnp.where(same, jnp.broadcast_to(loss_sum, (size, size)), 0.0), axis=0, keepdims=True)
    text_unit, text_norm = kept["text"]
    total = jnp.zeros((size, width), F32)
    for at, copy in back_copies.items():
        copy.wait_recv()
        total = total + text_got[at * size : (at + 1) * size, :].astype(F32)
    text_out[...] = back(total, text_unit, text_norm).astype(BF16)

    last = core_copies + list(side_copies.values()) + list(iback_copies.values()) + list(back_copies.values())
    for copy in row_copies + text_copies + image_copies + last:
        copy.wait_send()


def solution(mesh):
    depth = mesh.shape["blk"] // 4
    peers = mesh.shape["group"]
    image_far, text_far = offsets(depth)
    near = len(image_far)
    lines = len(text_far)

    def body(
        patches,
        patch_counts,
        dest_list,
        probe,
        w_attn_out,
        w_key,
        w_value,
        texts,
        image_labels,
        text_labels,
        log_temp,
        bias,
    ):
        rows, width = patches.shape
        size = texts.shape[0]
        padded = -(-rows // LANES) * LANES
        far = pl.BlockSpec(memory_space=pl.ANY)
        local = pl.BlockSpec(memory_space=pltpu.VMEM)
        dma = lambda n: pltpu.SemaphoreType.DMA((n,))
        image_grad, text_grad, row_loss = pl.pallas_call(
            functools.partial(kernel, depth, peers),
            out_shape=(
                pltpu.VMEM((size, width), BF16),
                pltpu.VMEM((size, width), BF16),
                pltpu.VMEM((1, size), F32),
            ),
            in_specs=[far] * 10 + [pl.BlockSpec(memory_space=pltpu.SMEM)] * 2,
            out_specs=(local, local, local),
            scratch_shapes=[
                pltpu.VMEM((1, peers), jnp.int32),
                pltpu.VMEM((1, peers), jnp.int32),
                pltpu.VMEM((width,), BF16),
                pltpu.VMEM((1, size), jnp.int32),
                pltpu.VMEM((1, size), jnp.int32),
                pltpu.VMEM((rows, width), BF16),
                pltpu.VMEM((width, width), BF16),
                pltpu.VMEM((width, width), BF16),
                pltpu.VMEM((width, width), BF16),
                pltpu.VMEM((size, width), BF16),
                pltpu.VMEM((padded, width), F32),
                pltpu.VMEM((peers, 1, width), F32),
                pltpu.VMEM((peers, 1, width), F32),
                pltpu.VMEM((size, width + LANES), BF16),
                pltpu.VMEM((2 * lines * size, width + LANES), BF16),
                pltpu.VMEM((2 * near * size, width + LANES), BF16),
                pltpu.VMEM((near * size, width + LANES), BF16),
                pltpu.VMEM((near * size, width + LANES), BF16),
                pltpu.VMEM((near * size, width + LANES), BF16),
                pltpu.VMEM((near * size, width + LANES), BF16),
                pltpu.VMEM((lines * size, width), BF16),
                pltpu.VMEM((lines * size, width), BF16),
                pltpu.VMEM((lines * size, width), BF16),
                pltpu.VMEM((lines * size, width), BF16),
                dma(7 + 3 * parts(width)),
                dma(peers),
                dma(peers),
                dma(lines + 1),
                dma(lines + 1),
                dma(2 * near),
                dma(2 * near),
                dma(near),
                dma(near),
                dma(lines),
                dma(lines),
                dma(lines),
                dma(lines),
                dma(near),
                dma(near),
            ],
            compiler_params=pltpu.CompilerParams(
                collective_id=0, has_side_effects=True, vmem_limit_bytes=62 * 1024 * 1024
            ),
            cost_estimate=pl.CostEstimate(
                flops=8 * rows * width * width, bytes_accessed=8 * width * width, transcendentals=0
            ),
            name="pool_and_contrast",
        )(
            patches,
            patch_counts,
            dest_list,
            probe,
            w_attn_out,
            w_key,
            w_value,
            texts,
            image_labels.reshape(1, size),
            text_labels.reshape(1, size),
            log_temp,
            bias,
        )
        return (image_grad, text_grad, row_loss.reshape(size))

    whole = P(("blk", "group"), None)
    flat = P(("blk", "group"))
    return jax.shard_map(
        body,
        mesh=mesh,
        in_specs=(whole, whole, whole, P(), P(), P(), P(), whole, flat, flat, P(), P()),
        out_specs=(whole, whole, flat),
        check_vma=False,
    )
```

```python
import functools

import jax
import jax.numpy as jnp
from jax import lax
from jax.experimental import pallas as pl
from jax.experimental.pallas import tpu as pltpu
from jax.sharding import PartitionSpec as P

HEADS = 16
LANES = 128
NEG = -1e30
F32 = jnp.float32
BF16 = jnp.bfloat16
NT = (((1,), (1,)), ((), ()))
TN = (((0,), (0,)), ((), ()))


def offsets(depth):
    if depth == 16:
        return ((0, 1, -1, 2), (-6, 6, -2, 2))
    if depth == 4:
        return ((0, 1), (-1, 1))
    raise ValueError("depth of z")


def parts(width):
    return 3 if width % (3 * LANES) == 0 else 1


def dot(a, b, dims=(((1,), (0,)), ((), ()))):
    return lax.dot_general(a, b, dims, preferred_element_type=F32)


def split(data, pieces):
    out = []
    for _ in range(pieces - 1):
        piece = data.astype(BF16)
        out.append(piece)
        data = data - piece.astype(F32)
    return out + [data.astype(BF16)]


def iota(shape, axis):
    return lax.broadcasted_iota(jnp.int32, shape, axis)


def column(row):
    n = row.shape[1]
    same = iota((n, n), 0) == iota((n, n), 1)
    return jnp.sum(jnp.where(same, jnp.broadcast_to(row, (n, n)), 0.0), axis=1, keepdims=True)


def unit(data):
    norm = jnp.sqrt(jnp.sum(data * data, axis=-1, keepdims=True) + 1e-06)
    return (data / norm, norm)


def back(grad, row_unit, norm):
    return (grad - row_unit * jnp.sum(row_unit * grad, axis=-1, keepdims=True)) / norm


def pool(patch, counts, dest, probe, key_w, proj_w, value_w, ready, normed):
    rows, width = patch.shape
    padded = normed.shape[0]
    head = width // HEADS
    images = counts.shape[1]
    cuts = parts(width)
    wide = width // cuts
    if padded > rows:
        normed[rows:padded, :] = jnp.zeros((padded - rows, width), F32)
    for cut in range(cuts):
        ready("proj", cut)
        normed[0:rows, cut * wide : (cut + 1) * wide] = dot(patch[...], proj_w[:, cut * wide : (cut + 1) * wide])
    proj = normed[0:rows, :]
    centre = proj - jnp.mean(proj, axis=-1, keepdims=True)
    normed[0:rows, :] = centre / jnp.sqrt(jnp.mean(centre * centre, axis=-1, keepdims=True) + 1e-06)
    low = iota((HEADS, width), 0) * head
    lane = iota((HEADS, width), 1)
    key_probe = []
    for cut in range(cuts):
        ready("key", cut)
        spread = jnp.where(
            (lane >= low) & (lane < low + head), jnp.broadcast_to(probe[...].astype(F32).reshape(1, width), (HEADS, width)), 0.0
        ).astype(BF16)
        key_probe.append(dot(spread, key_w[cut * wide : (cut + 1) * wide, :], NT))
    key_probe = jnp.concatenate(split(jnp.concatenate(key_probe, axis=1), 3), axis=0)
    pieces = split(normed[...], 2)
    scores = jnp.transpose(dot(pieces[1], key_probe, NT) + dot(pieces[0], key_probe, NT))
    scores = scores[:HEADS] + (scores[HEADS : 2 * HEADS] + scores[2 * HEADS : 3 * HEADS])
    scores = scores / jnp.sqrt(F32(head))
    image = iota((images, images), 0)
    which = iota((images, images), 1)
    lengths = jnp.broadcast_to(column(counts[...].astype(F32)), (images, images))
    first = jnp.sum(jnp.where(image < which, lengths, 0.0), axis=0, keepdims=True)
    last = jnp.sum(jnp.where(image <= which, lengths, 0.0), axis=0, keepdims=True)
    chosen = jnp.broadcast_to(dest[...], (images, images)) == image
    first = jnp.sum(jnp.where(chosen, jnp.broadcast_to(first, (images, images)), 0.0), axis=1, keepdims=True)
    last = jnp.sum(jnp.where(chosen, jnp.broadcast_to(last, (images, images)), 0.0), axis=1, keepdims=True)
    place = iota((images, padded), 1).astype(F32)
    member = ((place >= first) & (place < last))[None]
    masked = jnp.where(member, scores[:, None, :], NEG)
    expo = jnp.where(member, jnp.exp(masked - jnp.max(masked, axis=2, keepdims=True)), 0.0)
    weights = expo / jnp.sum(expo, axis=2, keepdims=True)
    weights = weights.reshape(HEADS * images, padded).astype(BF16)
    mixed = dot(weights, pieces[0]).astype(BF16)
    out = []
    for cut in range(cuts):
        ready("value", cut)
        first_head, last_head = cut * wide // head, -(-(cut + 1) * wide // head)
        taken = slice(first_head * images, last_head * images)
        full = dot(mixed[taken], value_w[:, cut * wide : (cut + 1) * wide])
        lane = iota((images, wide), 1) + cut * wide
        kept = jnp.zeros((images, wide), F32)
        for at in range(first_head, last_head):
            inside = (lane >= at * head) & (lane < at * head + head)
            kept = jnp.where(inside, full[(at - first_head) * images : (at - first_head + 1) * images], kept)
        out.append(kept)
    return jnp.concatenate(out, axis=1).astype(BF16).astype(F32)


def pairs(images, texts, width, temp, shift):
    logits = temp * dot(images[:, :width], texts[:, :width], NT) + shift
    apart = dot(images[:, width:], texts[:, width:], NT)
    signs = jnp.where(jnp.abs(apart) < 0.5, 1.0, -1.0).astype(F32)
    turned = -signs * logits
    small = jnp.exp(-jnp.abs(turned))
    loss = jnp.maximum(turned, 0.0) + jnp.log1p(small)
    sigmoid = jnp.where(turned >= 0, 1.0, small) / (1.0 + small)
    return (temp * -signs * sigmoid).astype(BF16), jnp.sum(loss, axis=1, keepdims=True)


def kernel(
    depth,
    peers,
    patches,
    counts_hbm,
    dest_hbm,
    probe_hbm,
    w_proj,
    w_key,
    w_value,
    texts,
    image_labels_hbm,
    text_labels_hbm,
    log_temp,
    bias,
    image_out,
    text_out,
    loss_out,
    counts,
    dest,
    probe,
    image_labels,
    text_labels,
    patch_buf,
    proj_buf,
    key_buf,
    value_buf,
    text_buf,
    normed,
    row_out,
    row_in,
    text_own,
    text_set,
    image_set,
    side_back,
    side_got,
    image_back,
    image_got,
    core_back,
    core_got,
    text_back,
    text_got,
    load_sem,
    row_send,
    row_recv,
    text_send,
    text_recv,
    image_send,
    image_recv,
    iback_send,
    iback_recv,
    tback_send,
    tback_recv,
    core_send,
    core_recv,
    side_send,
    side_recv,
):
    width = patches.shape[1]
    size = text_buf.shape[0]
    image_far, text_far = offsets(depth)
    reach = [(turn, far) for turn in (0, 1) for far in image_far]
    half = len(text_far) * size
    near = len(image_far)

    here = lax.axis_index("blk")
    mine = lax.axis_index("group")
    at_x, at_z, at_core = here // (2 * depth), (here // 2) % depth, here % 2
    way = 1 - 2 * at_core

    def blk(turn_x, far, turn_core):
        x = (at_x + turn_x) % 2
        z = (at_z + far + depth) % depth
        core = (at_core + turn_core) % 2
        return {"blk": (x * depth + z) * 2 + core}

    def remote(src, dst, send, recv, device):
        copy = pltpu.make_async_remote_copy(
            src_ref=src,
            dst_ref=dst,
            send_sem=send,
            recv_sem=recv,
            device_id=device,
            device_id_type=pl.DeviceIdType.MESH,
        )
        copy.start()
        return copy

    loads = {}

    def load(name, src, dst):
        loads[name] = pltpu.make_async_copy(src, dst, load_sem.at[len(loads)])
        loads[name].start()

    cuts = parts(width)
    wide = width // cuts
    load("patch", patches, patch_buf)
    for cut in range(cuts):
        some = pl.ds(cut * wide, wide)
        load(("proj", cut), w_proj.at[:, some], proj_buf.at[:, some])
    load("text", texts, text_buf)
    for name, src, dst in (
        ("counts", counts_hbm, counts),
        ("dest", dest_hbm, dest),
        ("probe", probe_hbm, probe),
        ("image_labels", image_labels_hbm, image_labels),
        ("text_labels", text_labels_hbm, text_labels),
    ):
        load(name, src, dst)
    for cut in range(cuts):
        some = pl.ds(cut * wide, wide)
        load(("key", cut), w_key.at[some, :], key_buf.at[some, :])
    for cut in range(cuts):
        some = pl.ds(cut * wide, wide)
        load(("value", cut), w_value.at[:, some], value_buf.at[:, some])

    known = {(turn, far % depth, 0) for turn, away in reach for far in (away, -away)}
    known |= {(0, far % depth, 0) for away in text_far for far in (away, -away)}
    known |= {(0, 0, 1)}
    known -= {(0, 0, 0)}
    barrier = pltpu.get_barrier_semaphore()
    for partner in sorted(known):
        pl.semaphore_signal(barrier, inc=1, device_id=blk(*partner), device_id_type=pl.DeviceIdType.MESH)
    for step in range(1, peers):
        pl.semaphore_signal(
            barrier, inc=1, device_id={"group": (mine + step) % peers}, device_id_type=pl.DeviceIdType.MESH
        )

    def block(ref, at, count=1):
        return ref.at[pl.ds(at * size, count * size), :]

    lane = iota((size, LANES), 1)
    loads["patch"].wait()
    text_copies = []
    kept = {}

    def ready(name, cut):
        loads[(name, cut)].wait()
        if name == "key" and cut == 0:
            for other in ("text", "counts", "dest", "probe", "image_labels", "text_labels"):
                loads[other].wait()
            text_unit, text_norm = unit(text_buf[...].astype(F32))
            kept["text"] = (text_unit, text_norm)
            text_own[:, 0:width] = text_unit.astype(BF16)
            text_label = column(text_labels[...].astype(F32))
            text_own[:, width:] = jnp.where(lane == 0, 1.0, jnp.where(lane == 1, -text_label, 0.0)).astype(BF16)
        if name == "value" and cut == 0:
            pl.semaphore_wait(barrier, len(known) + peers - 1)
            for at in range(len(text_far)):
                text_copies.append(
                    remote(
                        text_own,
                        block(text_set, at),
                        text_send.at[at],
                        text_recv.at[at],
                        blk(0, text_far[at], 0),
                    )
                )

    ordered = pool(patch_buf, counts, dest, probe, key_buf, proj_buf, value_buf, ready, normed)
    for at in range(peers):
        row_out[at] = ordered[at : at + 1, :]
    row_copies = []
    for step in sorted(range(1, peers), key=lambda step: abs(step - peers // 2)):
        to = (mine + step) % peers
        row_copies.append(
            remote(
                row_out.at[to], row_in.at[mine], row_send.at[step], row_recv.at[step], {"group": to}
            )
        )
    row_in[mine] = row_out[mine]
    image_label = column(image_labels[...].astype(F32))
    image_set[0:size, width:] = jnp.where(lane == 0, image_label, jnp.where(lane == 1, 1.0, 0.0)).astype(BF16)
    temp = jnp.exp(jnp.full((1, 1), log_temp[0], F32))
    for copy in row_copies:
        copy.wait_recv()
    placed = jnp.concatenate([row_in[at] for at in range(peers)], axis=0)
    image_unit, image_norm = unit(placed)
    image_set[0:size, 0:width] = image_unit.astype(BF16)
    image_copies = []
    for at in sorted(range(1, len(reach)), key=lambda at: -abs(reach[at][1])):
        image_copies.append(
            remote(
                block(image_set, 0),
                block(image_set, at),
                image_send.at[at],
                image_recv.at[at],
                blk(reach[at][0], way * reach[at][1], 0),
            )
        )
    for copy in text_copies:
        copy.wait_recv()
    text_copies.append(
        remote(
            text_set.at[pl.ds(0, half), :],
            text_set.at[pl.ds(half, half), :],
            text_send.at[len(text_far)],
            text_recv.at[len(text_far)],
            blk(0, 0, 1),
        )
    )
    text_copies[-1].wait_recv()
    for copy in image_copies:
        copy.wait_recv()

    weights, loss = pairs(image_set[...], text_set[...], width, temp, jnp.full((1, 1), bias[0], F32))
    core_back[...] = dot(weights[:, half:], image_set[:, :width], TN).astype(BF16)
    core_copies = [
        remote(block(core_back, at), block(core_got, at), core_send.at[at], core_recv.at[at], blk(0, 0, 1))
        for at in range(len(text_far))
    ]

    def tails(data):
        wide_lane = iota((data.shape[0], LANES), 1)
        high, low = split(data, 2)
        return jnp.where(
            wide_lane == 0, high.astype(F32), jnp.where(wide_lane == 1, low.astype(F32), 0.0)
        ).astype(BF16)

    def tail(data):
        return jnp.sum(data.astype(F32), axis=1, keepdims=True)

    side_back[:, 0:width] = dot(weights[near * size :], text_set[:, :width]).astype(BF16)
    side_back[:, width:] = tails(loss[near * size :])
    order = sorted(range(near), key=lambda at: -abs(image_far[at]))
    side_copies = {}
    for at in order:
        side_copies[at] = remote(
            block(side_back, at),
            block(side_got, at),
            side_send.at[at],
            side_recv.at[at],
            blk(1, -way * image_far[at], 0),
        )
    text_part = dot(weights[:, :half], image_set[:, :width], TN)
    image_part = dot(weights[: near * size], text_set[:, :width])
    back_copies = {}
    for at in range(len(text_far)):
        core_copies[at].wait_recv()
        rows = slice(at * size, (at + 1) * size)
        text_back[rows, :] = (text_part[rows] + core_got[rows, :].astype(F32)).astype(BF16)
        back_copies[at] = remote(
            block(text_back, at),
            block(text_got, at),
            tback_send.at[at],
            tback_recv.at[at],
            blk(0, -text_far[at], 0),
        )
    image_back[:, 0:width] = image_part.astype(BF16)
    image_back[:, width:] = tails(loss[: near * size])
    iback_copies = {}
    for at in order:
        if image_far[at]:
            iback_copies[at] = remote(
                block(image_back, at),
                block(image_got, at),
                iback_send.at[at],
                iback_recv.at[at],
                blk(0, -way * image_far[at], 0),
            )
    image_sum = image_part[:size]
    loss_sum = loss[:size]
    for got, copies in ((side_got, side_copies), (image_got, iback_copies)):
        for at, copy in copies.items():
            copy.wait_recv()
            rows = slice(at * size, (at + 1) * size)
            image_sum = image_sum + got[rows, :width].astype(F32)
            loss_sum = loss_sum + tail(got[rows, width:])
    image_out[...] = back(image_sum, image_unit, image_norm).astype(BF16)
    loss_sum = loss_sum / F32(len(reach) * len(text_far) * 2 * size)
    same = iota((size, size), 0) == iota((size, size), 1)
    loss_out[...] = jnp.sum(jnp.where(same, jnp.broadcast_to(loss_sum, (size, size)), 0.0), axis=0, keepdims=True)
    text_unit, text_norm = kept["text"]
    total = jnp.zeros((size, width), F32)
    for at, copy in back_copies.items():
        copy.wait_recv()
        total = total + text_got[at * size : (at + 1) * size, :].astype(F32)
    text_out[...] = back(total, text_unit, text_norm).astype(BF16)

    last = core_copies + list(side_copies.values()) + list(iback_copies.values()) + list(back_copies.values())
    for copy in row_copies + text_copies + image_copies + last:
        copy.wait_send()


def solution(mesh):
    depth = mesh.shape["blk"] // 4
    peers = mesh.shape["group"]
    image_far, text_far = offsets(depth)
    near = len(image_far)
    lines = len(text_far)

    def body(
        patches,
        patch_counts,
        dest_list,
        probe,
        w_attn_out,
        w_key,
        w_value,
        texts,
        image_labels,
        text_labels,
        log_temp,
        bias,
    ):
        rows, width = patches.shape
        size = texts.shape[0]
        padded = -(-rows // LANES) * LANES
        far = pl.BlockSpec(memory_space=pl.ANY)
        local = pl.BlockSpec(memory_space=pltpu.VMEM)
        dma = lambda n: pltpu.SemaphoreType.DMA((n,))
        image_grad, text_grad, row_loss = pl.pallas_call(
            functools.partial(kernel, depth, peers),
            out_shape=(
                pltpu.VMEM((size, width), BF16),
                pltpu.VMEM((size, width), BF16),
                pltpu.VMEM((1, size), F32),
            ),
            in_specs=[far] * 10 + [pl.BlockSpec(memory_space=pltpu.SMEM)] * 2,
            out_specs=(local, local, local),
            scratch_shapes=[
                pltpu.VMEM((1, peers), jnp.int32),
                pltpu.VMEM((1, peers), jnp.int32),
                pltpu.VMEM((width,), BF16),
                pltpu.VMEM((1, size), jnp.int32),
                pltpu.VMEM((1, size), jnp.int32),
                pltpu.VMEM((rows, width), BF16),
                pltpu.VMEM((width, width), BF16),
                pltpu.VMEM((width, width), BF16),
                pltpu.VMEM((width, width), BF16),
                pltpu.VMEM((size, width), BF16),
                pltpu.VMEM((padded, width), F32),
                pltpu.VMEM((peers, 1, width), F32),
                pltpu.VMEM((peers, 1, width), F32),
                pltpu.VMEM((size, width + LANES), BF16),
                pltpu.VMEM((2 * lines * size, width + LANES), BF16),
                pltpu.VMEM((2 * near * size, width + LANES), BF16),
                pltpu.VMEM((near * size, width + LANES), BF16),
                pltpu.VMEM((near * size, width + LANES), BF16),
                pltpu.VMEM((near * size, width + LANES), BF16),
                pltpu.VMEM((near * size, width + LANES), BF16),
                pltpu.VMEM((lines * size, width), BF16),
                pltpu.VMEM((lines * size, width), BF16),
                pltpu.VMEM((lines * size, width), BF16),
                pltpu.VMEM((lines * size, width), BF16),
                dma(7 + 3 * parts(width)),
                dma(peers),
                dma(peers),
                dma(lines + 1),
                dma(lines + 1),
                dma(2 * near),
                dma(2 * near),
                dma(near),
                dma(near),
                dma(lines),
                dma(lines),
                dma(lines),
                dma(lines),
                dma(near),
                dma(near),
            ],
            compiler_params=pltpu.CompilerParams(
                collective_id=0, has_side_effects=True, vmem_limit_bytes=62 * 1024 * 1024
            ),
            cost_estimate=pl.CostEstimate(
                flops=8 * rows * width * width, bytes_accessed=8 * width * width, transcendentals=0
            ),
            name="pool_and_contrast",
        )(
            patches,
            patch_counts,
            dest_list,
            probe,
            w_attn_out,
            w_key,
            w_value,
            texts,
            image_labels.reshape(1, size),
            text_labels.reshape(1, size),
            log_temp,
            bias,
        )
        return (image_grad, text_grad, row_loss.reshape(size))

    whole = P(("blk", "group"), None)
    flat = P(("blk", "group"))
    return jax.shard_map(
        body,
        mesh=mesh,
        in_specs=(whole, whole, whole, P(), P(), P(), P(), whole, flat, flat, P(), P()),
        out_specs=(whole, whole, flat),
        check_vma=False,
    )
```
